256 devices in a mesh: tile: 64 (over z_lo, y, x), slab: 4 (over z_hi, core).
Axes of the slice: x: 4, y: 4, z: 8 (z_hi: 2, z_lo: 4; z = z_hi * 4 + z_lo), core: 2. Of those that a mesh axis runs over, the one named last changes fastest.
Arguments:
- old_conc: float32 [32, 512, 32, 128], P(None, 'tile', 'slab'), may hold values from -6 to 6
- upwind: bfloat16 [512, 32, 3, 128, 128], P('tile', 'slab'), may hold values from -0.09375 to 0.09375
- diag_inverse: bfloat16 [512, 32, 128, 128], P('tile', 'slab')
- neighbours: int32 [512, 32, 3], P('tile', 'slab'), may hold values from 0 to 99, as said below
- streams: float32 [64, 32, 128], P('tile'), may hold values from -6 to 6
- injector_row: int32 [64], replicated, may hold values from 0 to 63, each once
- perf_well: int32 [64, 4, 4], P('tile', 'slab'), may hold values from 0 to 63
- perf_block: int32 [64, 4, 4], P('tile', 'slab'), may hold values from 0 to 63
- perf_rate: float32 [64, 4, 4], P('tile', 'slab'), may hold values from 0.5 to 2
Outputs:
- new_conc: float32 [32, 512, 32, 128], P(None, 'tile', 'slab')
The draws below stay inside these ranges and needn't reach their ends.
Inputs may be any that keep to these rules, and one draw needn't show every extreme that they name: `neighbours`: indices into a grid of (10) x (10) blocks, row-major, each within one block of its own block in both directions, never the block itself. `injector_row`: each row of streams is named by exactly one well.
All inputs are finite; a program needn't handle non-finite values.
Results may differ from the reference program's by a relative error of at most 0.0045.
Values may be sent and summed in bfloat16 or wider, within the bound.
No kernel may reach another device: no remote copies, remote signals or barrier semaphores. Data moves between devices by JAX's collectives and lax.ppermute only.
A program may use at most 64 MiB of HBM per device.

```python
import math
import jax
import jax.numpy as jnp
from jax import lax

TRACERS = 32
CELLS = 128
K = 3
SWEEPS = 3
BT = 8
BS = 8
PERF = 4
NBT = 512
NBS = 32
WELLS = 64
N_TILE = 64
N_SLAB = 4


def draw_neighbours(key, part):
    key = jax.random.fold_in(key, 11)
    direction = jax.random.randint(key, (NBT, NBS, K), 0, 8)
    compass = direction + (direction >= 4).astype(jnp.int32)
    row_step = compass // 3 - 1
    col_step = compass % 3 - 1
    local_row = (jnp.arange(NBT, dtype=jnp.int32) % BT)[:, None, None]
    local_col = (jnp.arange(NBS, dtype=jnp.int32) % BS)[None, :, None]
    target = (local_row + 1 + row_step) * (BS + 2) + local_col + 1 + col_step
    first_slot = (jnp.arange(K, dtype=jnp.int32) == 0)[None, None, :]
    target = jnp.where(first_slot & (local_row == 0) & (local_col == 0), 0, target)
    target = jnp.where(first_slot & (local_row == BT - 1) & (local_col == BS - 1), (BT + 2) * (BS + 2) - 1, target)
    return target.astype(jnp.int32)


def draw_diag_inverse(key, part):
    key = jax.random.fold_in(key, 12)
    first_key, second_key = jax.random.split(key)
    scale = jax.random.uniform(first_key, (NBT, NBS, CELLS, 1), jnp.float32, 0.5, 1.0)
    spread = jax.random.normal(second_key, (NBT, NBS, CELLS, CELLS), jnp.float32)
    block = jnp.eye(CELLS, dtype=jnp.float32) * scale + spread * (0.2 / math.sqrt(CELLS))
    return block.astype(jnp.bfloat16)


def place_ends(array, own_key, smallest, top_value):
    spot = [jax.random.randint(jax.random.fold_in(own_key, axis), (), 0, length) for axis, length in enumerate(array.shape)]
    main_axis = array.shape.index(max(array.shape))
    neighbour = spot[:main_axis] + [(spot[main_axis] + 1) % array.shape[main_axis]] + spot[main_axis + 1:]
    return array.at[tuple(spot)].set(smallest).at[tuple(neighbour)].set(top_value)


def block_levels(own_key, dims, cuts, smallest, largest):
    gain = 1.0
    for axis_at, parts in cuts:
        steps = jax.random.uniform(jax.random.fold_in(jax.random.fold_in(own_key, 6), axis_at), (parts,), jnp.float32, smallest / len(cuts), largest / len(cuts))
        gain = gain * jnp.repeat(jnp.exp(steps), dims[axis_at] // parts).reshape((-1,) + (1,) * (len(dims) - 1 - axis_at))
    return gain


def gaussian(stream_key, dims, width, limit, pieces=(), kind=jnp.bfloat16):
    level = block_levels(stream_key, dims, pieces, -0.22, 0.18) if pieces else 1.0
    values = jax.random.normal(stream_key, dims, jnp.float32) * width * level
    return jnp.minimum(jnp.maximum(values, -limit), limit).astype(kind)


def setup_inputs(seed: int = 0) -> dict:
    keys = jax.random.split(jax.random.key(seed), 10)
    return {
        "old_conc": gaussian(keys[0], (TRACERS, NBT, NBS, CELLS), 1.0, 6.0, ((1, 64), (2, 4)), jnp.float32),
        "upwind": gaussian(keys[1], (NBT, NBS, K, CELLS, CELLS), (TRACERS * CELLS) ** -0.5, 0.09375, ((0, 64), (1, 4))),
        "diag_inverse": draw_diag_inverse(jax.random.fold_in(keys[9], 71), 0),
        "neighbours": draw_neighbours(jax.random.fold_in(keys[9], 71), 0),
        "streams": gaussian(keys[4], (WELLS, TRACERS, CELLS), 1.0, 6.0, ((0, 64),), jnp.float32),
        "injector_row": jax.random.permutation(keys[5], WELLS).astype(jnp.int32),
        "perf_well": place_ends(jax.random.randint(keys[6], (N_TILE, N_SLAB, PERF), 0, WELLS), jax.random.fold_in(keys[6], 1), 0, WELLS - 1).astype(jnp.int32),
        "perf_block": place_ends(jax.random.randint(keys[7], (N_TILE, N_SLAB, PERF), 0, BT * BS), jax.random.fold_in(keys[7], 1), 0, (BT * BS) - 1).astype(jnp.int32),
        "perf_rate": jnp.clip(jnp.exp(math.log(2.0) - 1.3862944 * jax.random.uniform(keys[8], (N_TILE, N_SLAB, PERF), jnp.float32) ** block_levels(keys[8], (N_TILE, N_SLAB, PERF), ((0, 64), (1, 4)), -0.2, 0.2)), 0.5, 2.0),
    }


def reference(old_conc, upwind, diag_inverse, neighbours, streams, injector_row, perf_well, perf_block, perf_rate):
    picked = streams[injector_row[perf_well]]
    tile_ids = jnp.arange(N_TILE, dtype=jnp.int32)[:, None, None]
    slab_ids = jnp.arange(N_SLAB, dtype=jnp.int32)[None, :, None]
    row_index = tile_ids * BT + perf_block // BS
    col_index = slab_ids * BS + perf_block % BS
    added = perf_rate[..., None, None] * picked
    rhs = old_conc.at[:, row_index, col_index, :].add(jnp.moveaxis(added, 3, 0))
    row_base = (jnp.arange(NBT, dtype=jnp.int32) // BT * BT)[:, None, None]
    col_base = (jnp.arange(NBS, dtype=jnp.int32) // BS * BS)[None, :, None]
    global_row = row_base + neighbours // (BS + 2)
    global_col = col_base + neighbours % (BS + 2)
    concentration = old_conc
    for sweep_index in range(SWEEPS):
        rounded = concentration.astype(jnp.bfloat16)
        padded = jnp.pad(rounded, ((0, 0), (1, 1), (1, 1), (0, 0)))

        def one_row(row_at):
            upstream = padded[:, global_row[row_at], global_col[row_at], :].astype(jnp.float32)
            coupled = jnp.einsum('tbkj,bkij->tbi', upstream, upwind[row_at].astype(jnp.float32), precision=lax.Precision.HIGHEST)
            remainder = (rhs[:, row_at] - coupled).astype(jnp.bfloat16)
            return jnp.einsum('tbj,bij->tbi', remainder.astype(jnp.float32), diag_inverse[row_at].astype(jnp.float32), precision=lax.Precision.HIGHEST)

        concentration = jnp.moveaxis(lax.map(one_row, jnp.arange(NBT, dtype=jnp.int32)), 0, 1)
    return concentration
```

```python
import functools

import jax
import jax.numpy as jnp
from jax import lax
from jax.experimental import pallas as pl
from jax.experimental.pallas import tpu as pltpu
from jax.sharding import PartitionSpec as P

BF16 = jnp.bfloat16
F32 = jnp.float32
BATCH = 16
WIDE = 10

dot_t = functools.partial(
    lax.dot_general,
    dimension_numbers=(((1,), (1,)), ((), ())),
    preferred_element_type=F32,
)


def place():
    slab = lax.axis_index("slab")
    return lax.axis_index("tile"), slab, lax.rem(slab, 2)


def edge_columns(parity):
    return 7 * (1 - parity), 7 * parity


def far_is_real(slab):
    return jnp.logical_or(slab == 1, slab == 2)


def only_if(real, value):
    return jnp.where(real, value, jnp.zeros_like(value))


def prepare(old, x, base, to_near, to_far):
    _, _, parity = place()
    near, far = edge_columns(parity)
    for b in range(64):
        block = old[pl.ds(b, 32, stride=64), :]
        base[b] = block
        x[b] = block.astype(BF16)
    for r in range(8):
        to_near[r] = x[r * 8 + near]
        to_far[r] = x[r * 8 + far]


def rows_to_send(x, from_near, from_far, to_below, to_above):
    _, slab, parity = place()
    near, far = 9 * (1 - parity), 9 * parity
    real = far_is_real(slab)
    for out, r in ((to_below, 7), (to_above, 0)):
        out[pl.ds(1, 8)] = x[pl.ds(8 * r, 8)]
        out[near] = from_near[r]
        out[far] = only_if(real, from_far[r])


def widen(grid, x, from_near, from_far, from_above, from_below):
    tile, slab, parity = place()
    near, far = 9 * (1 - parity), 9 * parity
    real = far_is_real(slab)
    grid[pl.ds(0, WIDE)] = only_if(tile > 0, from_above[...])
    grid[pl.ds(90, WIDE)] = only_if(tile < lax.axis_size("tile") - 1, from_below[...])
    for r in range(8):
        grid[pl.ds((r + 1) * WIDE + 1, 8)] = x[pl.ds(8 * r, 8)]
        grid[(r + 1) * WIDE + near] = from_near[r]
        grid[(r + 1) * WIDE + far] = only_if(real, from_far[r])


def sweep(neighbour, grid, rhs, upwind, diag, store):
    @pl.loop(0, 64 // BATCH)
    def _(step):
        first = step * BATCH
        remainders = []
        for q in range(BATCH):
            b = first + q
            upstream = jnp.concatenate([grid[neighbour[3 * b + k]] for k in range(3)], axis=1)
            weights = jnp.concatenate([upwind[b, k] for k in range(3)], axis=1)
            remainders.append((rhs[b] - dot_t(upstream, weights)).astype(BF16))
        for q in range(0, BATCH, 2):
            b = first + q
            both = jnp.concatenate(remainders[q : q + 2], axis=0)
            conc = dot_t(both, diag[pl.ds(b, 2)].reshape(256, 128))
            store(b, conc[:32, :128])
            store(b + 1, conc[32:, 128:])


def send_edges(x, to_near, to_far):
    _, _, parity = place()
    near, far = edge_columns(parity)
    for r in range(8):
        to_near[r] = x[r * 8 + near]
        to_far[r] = x[r * 8 + far]


def first_sweep(
    neighbour, slot_row, slot_block, slot_rate,
    x, from_near, from_far, from_above, from_below, base, rows, upwind, diag,
    x_next, to_near, to_far, rhs, grid,
):
    widen(grid, x, from_near, from_far, from_above, from_below)
    rhs[...] = base[...]
    for p in range(4):
        b = slot_block[p]
        rhs[b] = rhs[b] + slot_rate[p] * rows[slot_row[p]].astype(F32)

    def store(b, conc):
        x_next[b] = conc.astype(BF16)

    sweep(neighbour, grid, rhs, upwind, diag, store)
    send_edges(x_next, to_near, to_far)


def middle_sweep(
    neighbour, x, from_near, from_far, from_above, from_below, rhs, upwind, diag,
    x_next, to_near, to_far, grid,
):
    widen(grid, x, from_near, from_far, from_above, from_below)

    def store(b, conc):
        x_next[b] = conc.astype(BF16)

    sweep(neighbour, grid, rhs, upwind, diag, store)
    send_edges(x_next, to_near, to_far)


def last_sweep(
    neighbour, x, from_near, from_far, from_above, from_below, rhs, upwind, diag,
    out, grid,
):
    widen(grid, x, from_near, from_far, from_above, from_below)

    def store(b, conc):
        out[pl.ds(b, 32, stride=64), :] = conc

    sweep(neighbour, grid, rhs, upwind, diag, store)


def call(kernel, outs, scalars, arrays, scratch=(), flops=0):
    vmem = pl.BlockSpec(memory_space=pltpu.VMEM)
    smem = pl.BlockSpec(memory_space=pltpu.SMEM)
    return pl.pallas_call(
        kernel,
        out_shape=outs,
        in_specs=[smem] * len(scalars) + [vmem] * len(arrays),
        out_specs=[vmem] * len(outs),
        scratch_shapes=list(scratch),
        compiler_params=pltpu.CompilerParams(vmem_limit_bytes=32 * 2**20),
    )(*scalars, *arrays)


def blocks(count, dtype=BF16):
    return jax.ShapeDtypeStruct((count, 32, 128), dtype)


def body(
    old_conc, upwind, diag_inverse, neighbours, streams, injector_row, perf_well, perf_block, perf_rate
):
    tiles, slabs = lax.axis_size("tile"), lax.axis_size("slab")
    on_chip = [(s, s ^ 1) for s in range(slabs)]
    far_pairs = []
    for t in range(tiles):
        for s in range(slabs):
            to = (t, 3 - s) if s in (1, 2) else (t ^ 1, s)
            far_pairs.append((t * slabs + s, to[0] * slabs + to[1]))
    down = [(t, (t + 1) % tiles) for t in range(tiles)]
    up = [((t + 1) % tiles, t) for t in range(tiles)]

    def exchange(x, to_near, to_far):
        from_far = lax.ppermute(to_far, ("tile", "slab"), far_pairs)
        from_near = lax.ppermute(to_near, "slab", on_chip)
        to_below, to_above = call(rows_to_send, [blocks(10)] * 2, [], [x, from_near, from_far])
        from_above = lax.ppermute(to_below, "tile", down)
        from_below = lax.ppermute(to_above, "tile", up)
        return x, from_near, from_far, from_above, from_below

    old = old_conc.reshape(32 * 64, 128)
    upwind = pltpu.with_memory_space_constraint(upwind.reshape(64, 3, 128, 128), pltpu.VMEM)
    diag = pltpu.with_memory_space_constraint(diag_inverse.reshape(64, 128, 128), pltpu.VMEM)
    neighbour = neighbours.reshape(-1)
    slot_row = injector_row[perf_well.reshape(-1)]
    grid = pltpu.VMEM((100, 32, 128), BF16)

    x, base, to_near, to_far = call(prepare, [blocks(64), blocks(64, F32), blocks(8), blocks(8)], [], [old])
    everyone = jnp.broadcast_to(streams.astype(BF16), (tiles, 32, 128))
    rows = lax.all_to_all(everyone, "tile", 0, 0)
    x, to_near, to_far, rhs = call(
        first_sweep,
        [blocks(64), blocks(8), blocks(8), blocks(64, F32)],
        [neighbour, slot_row, perf_block.reshape(-1), perf_rate.reshape(-1)],
        [*exchange(x, to_near, to_far), base, rows, upwind, diag],
        [grid],
    )
    x, to_near, to_far = call(
        middle_sweep,
        [blocks(64), blocks(8), blocks(8)],
        [neighbour],
        [*exchange(x, to_near, to_far), rhs, upwind, diag],
        [grid],
    )
    (out,) = call(
        last_sweep,
        [jax.ShapeDtypeStruct((2048, 128), F32)],
        [neighbour],
        [*exchange(x, to_near, to_far), rhs, upwind, diag],
        [grid],
    )
    return out.reshape(old_conc.shape)


def solution(mesh):
    in_specs = (
        P(None, "tile", "slab", None),
        P("tile", "slab", None, None, None),
        P("tile", "slab", None, None),
        P("tile", "slab", None),
        P("tile", None, None),
        P(),
        P("tile", "slab", None),
        P("tile", "slab", None),
        P("tile", "slab", None),
    )
    out_specs = P(None, "tile", "slab", None)
    return jax.shard_map(body, mesh=mesh, in_specs=in_specs, out_specs=out_specs, check_vma=False)
```

```python
import functools

import jax
import jax.numpy as jnp
from jax import lax
from jax.experimental import pallas as pl
from jax.experimental.pallas import tpu as pltpu
from jax.sharding import PartitionSpec as P

BF16 = jnp.bfloat16
F32 = jnp.float32
WIDE = 10
CORNERS = (0, 7, 56, 63)
CORNER_HALOS = (0, 9, 90, 99)
INNER = tuple(b for b in range(64) if b not in CORNERS)

dot_t = functools.partial(
    lax.dot_general,
    dimension_numbers=(((1,), (1,)), ((), ())),
    preferred_element_type=F32,
)


def parity():
    return lax.rem(lax.axis_index("slab"), 2)


def even_tile():
    return lax.rem(lax.axis_index("tile"), 2) == 0


def far_is_real():
    slab = lax.axis_index("slab")
    return jnp.logical_or(slab == 1, slab == 2)


def above_is_real():
    return lax.axis_index("tile") > 0


def below_is_real():
    return lax.axis_index("tile") < lax.axis_size("tile") - 1


def only_if(real, value):
    return jnp.where(real, value, jnp.zeros_like(value))


def send_edges(x, to_near, to_far, to_mate, to_other):
    right, even = parity() == 0, even_tile()
    for r in range(8):
        first, last = x(r * 8), x(r * 8 + 7)
        to_near[r] = jnp.where(right, last, first)
        to_far[r] = jnp.where(right, first, last)
        top, bottom = x(r), x(56 + r)
        to_mate[r] = jnp.where(even, bottom, top)
        to_other[r] = jnp.where(even, top, bottom)


def bring_old(old, held, sems):
    copies = []
    for r in range(8):
        part = pl.ds(8 * r, 8)
        copies.append(pltpu.make_async_copy(old.at[:, part], held.at[:, part], sems.at[r]))
        copies[-1].start()
    return copies


def prepare(old, stream, x, everyone, to_near, to_far, to_mate, to_other, held, sems):
    copies = bring_old(old, held, sems)
    row = stream[0].astype(BF16)
    for t in range(everyone.shape[0]):
        everyone[t] = row
    rows = held.reshape(32 * 64, 128)
    for r in range(8):
        copies[r].wait()
        for b in range(8 * r, 8 * r + 8):
            x[b] = rows[pl.ds(b, 32, stride=64), :].astype(BF16)
    send_edges(lambda b: x[b], to_near, to_far, to_mate, to_other)


def pass_corners(from_near, from_far, to_mate, to_other):
    right, even = parity() == 0, even_tile()
    real = far_is_real()
    ends = []
    for r in (0, 7):
        near, far = from_near[r], only_if(real, from_far[r])
        ends.append((jnp.where(right, far, near), jnp.where(right, near, far)))
    for i in range(2):
        top, bottom = ends[0][i], ends[1][i]
        to_mate[i] = jnp.where(even, bottom, top)
        to_other[i] = jnp.where(even, top, bottom)


def widen(grid, x, corners, from_near, from_far, from_mate, from_other):
    right, even = parity() == 0, even_tile()
    real, above, below = far_is_real(), above_is_real(), below_is_real()
    for r in range(8):
        near, far = from_near[r], only_if(real, from_far[r])
        grid[(r + 1) * WIDE] = jnp.where(right, far, near)
        grid[(r + 1) * WIDE + 9] = jnp.where(right, near, far)
        mate, other = from_mate[r], from_other[r]
        grid[1 + r] = only_if(above, jnp.where(even, other, mate))
        grid[91 + r] = only_if(below, jnp.where(even, mate, other))
        grid[pl.ds((r + 1) * WIDE + 1, 8)] = x[pl.ds(8 * r, 8)]
    if corners is not None:
        for i, b in enumerate(CORNERS):
            grid[(b // 8 + 1) * WIDE + b % 8 + 1] = corners[i]


def sweep(ids, upstream, rhs, upwind, diag, store):
    remainders = []
    for b in ids:
        weights = jnp.concatenate([upwind[b, k] for k in range(3)], axis=1)
        remainders.append((rhs[b] - dot_t(upstream(b), weights)).astype(BF16))
    for i in range(0, len(ids), 2):
        both = jnp.concatenate(remainders[i : i + 2], axis=0)
        weights = jnp.concatenate([diag[ids[i]], diag[ids[i + 1]]], axis=0)
        conc = dot_t(both, weights)
        store(ids[i], conc[:32, :128])
        store(ids[i + 1], conc[32:, 128:])


def sweep_inner(neighbour, grid, rhs, upwind, diag, store, before=None, after=None):
    def upstream(b):
        return jnp.concatenate([grid[neighbour[3 * b + k]] for k in range(3)], axis=1)

    for r in range(0, 8, 2):
        if before is not None:
            before(r)
        sweep([b for b in range(8 * r, 8 * r + 16) if b in INNER], upstream, rhs, upwind, diag, store)
        if after is not None:
            after(r)


def inner_first(
    neighbour, well, row, where, rate, x, near, far, mate, other, rows, old, upwind_far, diag_far,
    x_next, grid, rhs, upwind, diag, held, old_sems, sems,
):
    old_copies = bring_old(old, held, old_sems)
    copies = []
    for r in range(0, 8, 2):
        part = pl.ds(8 * r, 16)
        copies.append(pltpu.make_async_copy(upwind_far.at[part], upwind.at[part], sems.at[r]))
        copies.append(pltpu.make_async_copy(diag_far.at[part], diag.at[part], sems.at[r + 1]))
    for copy in copies:
        copy.start()
    widen(grid, x, None, near, far, mate, other)
    for copy in old_copies:
        copy.wait()
    old_rows = held.reshape(32 * 64, 128)
    for b in range(64):
        rhs[b] = old_rows[pl.ds(b, 32, stride=64), :]
    for p in range(4):
        b = where[0, 0, p]
        rhs[b] = rhs[b] + rate[0, 0, p] * rows[row[well[0, 0, p]]].astype(F32)

    def store(b, conc):
        x_next[b] = conc.astype(BF16)

    def before(r):
        copies[r].wait()
        copies[r + 1].wait()

    sweep_inner(neighbour, grid, rhs, upwind, diag, store, before)


def inner(neighbour, x, corners, near, far, mate, other, rhs, upwind, diag, x_next, grid):
    widen(grid, x, corners, near, far, mate, other)

    def store(b, conc):
        x_next[b] = conc.astype(BF16)

    sweep_inner(neighbour, grid, rhs, upwind, diag, store)


def sweep_corners(neighbour, grid, mate, other, rhs, upwind, diag, store):
    even, above, below = even_tile(), above_is_real(), below_is_real()
    halos = [only_if(above, jnp.where(even, other[i], mate[i])) for i in range(2)]
    halos += [only_if(below, jnp.where(even, mate[i], other[i])) for i in range(2)]

    def upstream(b):
        i = CORNERS.index(b)
        slots = [neighbour[3 * b + k] for k in range(3)]
        return jnp.concatenate([jnp.where(n == CORNER_HALOS[i], halos[i], grid[n]) for n in slots], axis=1)

    sweep(CORNERS, upstream, rhs, upwind, diag, store)


def outer(neighbour, x, grid, mate, other, rhs, upwind, diag, corners, to_near, to_far, to_mate, to_other):
    def store(b, conc):
        corners[CORNERS.index(b)] = conc.astype(BF16)

    sweep_corners(neighbour, grid, mate, other, rhs, upwind, diag, store)
    block = lambda b: corners[CORNERS.index(b)] if b in CORNERS else x[b]
    send_edges(block, to_near, to_far, to_mate, to_other)


def inner_last(
    neighbour, x, corners, near, far, mate, other, rhs, upwind, diag, out, ends, grid, held, sems
):
    widen(grid, x, corners, near, far, mate, other)
    rows = held.reshape(32 * 64, 128)
    copies = []

    def store(b, conc):
        rows[pl.ds(b, 32, stride=64), :] = conc

    def after(r):
        for s in (r, r + 1):
            part = pl.ds(8 * s, 8)
            if s in (0, 7):
                ends[:, pl.ds(0 if s == 0 else 8, 8)] = held[:, part]
            else:
                copies.append(pltpu.make_async_copy(held.at[:, part], out.at[:, part], sems.at[s]))
                copies[-1].start()

    sweep_inner(neighbour, grid, rhs, upwind, diag, store, after=after)
    for copy in copies:
        copy.wait()


def outer_last(neighbour, partial, grid, mate, other, rhs, upwind, diag, ends, out, held, sems):
    del partial
    held[...] = ends[...]
    rows = held.reshape(32 * 16, 128)

    def store(b, conc):
        rows[pl.ds(b if b < 8 else b - 48, 32, stride=16), :] = conc

    sweep_corners(neighbour, grid, mate, other, rhs, upwind, diag, store)
    copies = []
    for i, r in enumerate((0, 7)):
        copies.append(pltpu.make_async_copy(held.at[:, pl.ds(8 * i, 8)], out.at[:, pl.ds(8 * r, 8)], sems.at[i]))
        copies[-1].start()
    for copy in copies:
        copy.wait()


VMEM, SMEM, ANY, HBM = (pl.BlockSpec(memory_space=m) for m in (pltpu.VMEM, pltpu.SMEM, pl.ANY, pltpu.HBM))


def call(kernel, outs, args, scratch=(), aliases=None, flops=0, moved=0):
    values = []
    for where, value in args:
        if where is VMEM:
            value = pltpu.with_memory_space_constraint(value, pltpu.VMEM)
        if where is HBM:
            value = pltpu.with_memory_space_constraint(value, pltpu.HBM)
        values.append(value)
    shapes = [pltpu.VMEM(s.shape, s.dtype) if where is VMEM else s for where, s in outs]
    return pl.pallas_call(
        kernel,
        out_shape=shapes,
        in_specs=[where for where, _ in args],
        out_specs=[where for where, _ in outs],
        scratch_shapes=list(scratch),
        input_output_aliases=aliases or {},
        cost_estimate=pl.CostEstimate(flops=flops, bytes_accessed=moved, transcendentals=0),
        compiler_params=pltpu.CompilerParams(vmem_limit_bytes=6 * 2**20),
    )(*values)


def blocks(count, dtype=BF16):
    return VMEM, jax.ShapeDtypeStruct((count, 32, 128), dtype)


def body(
    old_conc, upwind, diag_inverse, neighbours, streams, injector_row, perf_well, perf_block, perf_rate
):
    tiles, slabs = lax.axis_size("tile"), lax.axis_size("slab")
    both = ("tile", "slab")
    on_chip = [(s, s ^ 1) for s in range(slabs)]
    far_pairs, mates, others = [], [], []
    for t in range(tiles):
        for s in range(slabs):
            here = t * slabs + s
            far_pairs.append((here, t * slabs + 3 - s if s in (1, 2) else (t ^ 1) * slabs + s))
            mates.append((here, (t ^ 1) * slabs + s))
            other = t - 1 if t % 2 == 0 else t + 1
            others.append((here, other * slabs + s if 0 <= other < tiles else t * slabs + (s ^ 1)))

    def vmem(*values):
        return [(VMEM, v) for v in values]

    def exchange(to_near, to_far, to_mate, to_other):
        from_far = lax.ppermute(to_far, both, far_pairs)
        from_near = lax.ppermute(to_near, "slab", on_chip)
        from_mate = lax.ppermute(to_mate, both, mates)
        from_other = lax.ppermute(to_other, both, others)
        return from_near, from_far, from_mate, from_other

    def exchange_corners(from_near, from_far):
        to_mate, to_other = call(pass_corners, [blocks(2)] * 2, vmem(from_near, from_far))
        return lax.ppermute(to_mate, both, mates), lax.ppermute(to_other, both, others)

    dma = pltpu.SemaphoreType.DMA
    held = pltpu.VMEM((32, 64, 128), F32)
    edges = [blocks(8)] * 4
    neighbour = (SMEM, neighbours.reshape(-1))
    old = (HBM, old_conc.reshape(32, 64, 128))
    work = dict(flops=2 * 64 * 4 * 32 * 128 * 128, moved=9 * 2**20)

    x, everyone, *sent = call(
        prepare, [blocks(64), blocks(tiles), *edges], [old, (VMEM, streams)], [held, dma((8,))], moved=4 * 2**20
    )
    rows = lax.all_to_all(everyone, "tile", 0, 0)
    got = exchange(*sent)
    ends = exchange_corners(*got[:2])
    upwind_shape = jax.ShapeDtypeStruct((64, 3, 128, 128), BF16)
    diag_shape = jax.ShapeDtypeStruct((64, 128, 128), BF16)
    wells = [(SMEM, perf_well), (SMEM, injector_row), (SMEM, perf_block), (SMEM, perf_rate)]
    x, grid, rhs, *weights = call(
        inner_first,
        [blocks(64), blocks(100), blocks(64, F32), (VMEM, upwind_shape), (VMEM, diag_shape)],
        [neighbour, *wells, *vmem(x, *got, rows), old]
        + [(HBM, upwind.reshape(upwind_shape.shape)), (HBM, diag_inverse.reshape(diag_shape.shape))],
        [held, dma((8,)), dma((8,))],
        **work,
    )
    for last in (False, True):
        corners, *sent = call(outer, [blocks(4), *edges], [neighbour, *vmem(x, grid, *ends, rhs, *weights)])
        got = exchange(*sent)
        ends = exchange_corners(*got[:2])
        args = [neighbour, *vmem(x, corners, *got, rhs, *weights)]
        if not last:
            x, grid = call(inner, [blocks(64), blocks(100)], args, **work)
    whole = (ANY, jax.ShapeDtypeStruct((32, 64, 128), F32))
    partial, border, grid = call(
        inner_last,
        [whole, (VMEM, jax.ShapeDtypeStruct((32, 16, 128), F32)), blocks(100)],
        args,
        [held, pltpu.SemaphoreType.DMA((8,))],
        **work,
    )
    (out,) = call(
        outer_last,
        [whole],
        [neighbour, (ANY, partial), *vmem(grid, *ends, rhs, *weights, border)],
        [pltpu.VMEM((32, 16, 128), F32), pltpu.SemaphoreType.DMA((2,))],
        {1: 0},
    )
    return out.reshape(old_conc.shape)


def solution(mesh):
    in_specs = (
        P(None, "tile", "slab", None),
        P("tile", "slab", None, None, None),
        P("tile", "slab", None, None),
        P("tile", "slab", None),
        P("tile", None, None),
        P(),
        P("tile", "slab", None),
        P("tile", "slab", None),
        P("tile", "slab", None),
    )
    out_specs = P(None, "tile", "slab", None)
    return jax.shard_map(body, mesh=mesh, in_specs=in_specs, out_specs=out_specs, check_vma=False)
```

```python
import functools

import jax
import jax.numpy as jnp
from jax import lax
from jax.experimental import pallas as pl
from jax.experimental.pallas import tpu as pltpu
from jax.sharding import PartitionSpec as P

BF16 = jnp.bfloat16
F32 = jnp.float32
WIDE = 10
CORNERS = (0, 7, 56, 63)
CORNER_HALOS = (0, 9, 90, 99)
INTERIOR = tuple(b for b in range(64) if 0 < b // 8 < 7 and 0 < b % 8 < 7)
EDGES = tuple(b for b in range(64) if b not in INTERIOR and b not in CORNERS)
PLANE = 16

dot_t = functools.partial(
    lax.dot_general,
    dimension_numbers=(((1,), (1,)), ((), ())),
    preferred_element_type=F32,
)


def parity():
    return lax.rem(lax.axis_index("slab"), 2)


def even_tile():
    return lax.rem(lax.axis_index("tile"), 2) == 0


def far_is_real():
    slab = lax.axis_index("slab")
    return jnp.logical_or(slab == 1, slab == 2)


def above_is_real():
    return lax.axis_index("tile") > 0


def below_is_real():
    return lax.axis_index("tile") < lax.axis_size("tile") - 1


def only_if(real, value):
    return jnp.where(real, value, jnp.zeros_like(value))


def send_edges(x, to_near, to_far, to_mate, to_other):
    right, even = parity() == 0, even_tile()
    for r in range(8):
        first, last = x(r * 8), x(r * 8 + 7)
        to_near[r] = jnp.where(right, last, first)
        to_far[r] = jnp.where(right, first, last)
        top, bottom = x(r), x(56 + r)
        to_mate[r] = jnp.where(even, bottom, top)
        to_other[r] = jnp.where(even, top, bottom)


def bring_old(old, held, sems):
    copies = []
    for r in range(8):
        part = pl.ds(8 * r, 8)
        copies.append(pltpu.make_async_copy(old.at[:, part], held.at[:, part], sems.at[r]))
        copies[-1].start()
    return copies


def spread(stream, everyone, held, sem):
    copy = pltpu.make_async_copy(stream, held, sem)
    copy.start()
    copy.wait()
    row = held[0].astype(BF16)
    for t in range(PLANE):
        everyone[t] = row


def prepare(old, x, to_near, to_far, held, sems):
    copies = bring_old(old, held, sems)
    rows = held.reshape(32 * 64, 128)
    right = parity() == 0
    for r in range(8):
        copies[r].wait()
        for b in range(8 * r, 8 * r + 8):
            x[b] = rows[pl.ds(b, 32, stride=64), :].astype(BF16)
        first, last = x[8 * r], x[8 * r + 7]
        to_near[r] = jnp.where(right, last, first)
        to_far[r] = jnp.where(right, first, last)


def rows_to_send(x, from_near, from_far, to_mate, to_other):
    right, even = parity() == 0, even_tile()
    real = far_is_real()
    rows = []
    for r in (0, 7):
        near, far = from_near[r], only_if(real, from_far[r])
        rows.append([jnp.where(right, far, near), *(x[8 * r + c] for c in range(8)), jnp.where(right, near, far)])
    for i in range(WIDE):
        top, bottom = rows[0][i], rows[1][i]
        to_mate[i] = jnp.where(even, bottom, top)
        to_other[i] = jnp.where(even, top, bottom)


def pass_corners(from_near, from_far, to_mate, to_other):
    right, even = parity() == 0, even_tile()
    real = far_is_real()
    ends = []
    for r in (0, 7):
        near, far = from_near[r], only_if(real, from_far[r])
        ends.append((jnp.where(right, far, near), jnp.where(right, near, far)))
    for i in range(2):
        top, bottom = ends[0][i], ends[1][i]
        to_mate[i] = jnp.where(even, bottom, top)
        to_other[i] = jnp.where(even, top, bottom)


def at(b):
    return (b // 8 + 1) * WIDE + b % 8 + 1


def widen(grid, from_near, from_far, from_mate, from_other):
    right, even = parity() == 0, even_tile()
    real, above, below = far_is_real(), above_is_real(), below_is_real()
    for r in range(8):
        near, far = from_near[r], only_if(real, from_far[r])
        grid[(r + 1) * WIDE] = jnp.where(right, far, near)
        grid[(r + 1) * WIDE + 9] = jnp.where(right, near, far)
    count = from_mate.shape[0]
    first = (WIDE - count) // 2
    for c in range(count):
        mate, other = from_mate[c], from_other[c]
        grid[first + c] = only_if(above, jnp.where(even, other, mate))
        grid[90 + first + c] = only_if(below, jnp.where(even, mate, other))


def sweep(ids, upstream, rhs, upwind, diag, store):
    remainders = []
    for b in ids:
        weights = jnp.concatenate([upwind[b, k] for k in range(3)], axis=1)
        remainders.append((rhs[b] - dot_t(upstream(b), weights)).astype(BF16))
    for i in range(0, len(ids), 2):
        both = jnp.concatenate(remainders[i : i + 2], axis=0)
        weights = jnp.concatenate([diag[ids[i]], diag[ids[i + 1]]], axis=0)
        conc = dot_t(both, weights)
        store(ids[i], conc[:32, :128])
        store(ids[i + 1], conc[32:, 128:])


def from_grid(neighbour, grid):
    return lambda b: jnp.concatenate([grid[neighbour[3 * b + k]] for k in range(3)], axis=1)


def row_of(well, near_rows):
    away = (well // PLANE) ^ (lax.axis_index("tile") // PLANE)
    row = near_rows[0][well % PLANE]
    for m in range(1, 4):
        row = jnp.where(away == m, near_rows[m][well % PLANE], row)
    return row.astype(F32)


def sweep_first(
    neighbour, well, row, where, rate, x, near, far, mate, other, rows0, rows1, rows2, rows3, old, upwind_far, diag_far,
    x_next, rhs, upwind, diag, to_near, to_far, to_mate, to_other, grid, held, old_sems, sems,
):
    old_copies = bring_old(old, held, old_sems)
    copies = []
    for r in range(8):
        part = pl.ds(8 * r, 8)
        copies.append(
            (
                pltpu.make_async_copy(upwind_far.at[part], upwind.at[part], sems.at[2 * r]),
                pltpu.make_async_copy(diag_far.at[part], diag.at[part], sems.at[2 * r + 1]),
            )
        )

    def start(r):
        for copy in copies[r]:
            copy.start()

    start(0)
    start(1)
    widen(grid, near, far, mate, other)
    for b in range(64):
        grid[at(b)] = x[b]
    old_rows = held.reshape(32 * 64, 128)
    for r in range(8):
        old_copies[r].wait()
        for b in range(8 * r, 8 * r + 8):
            rhs[b] = old_rows[pl.ds(b, 32, stride=64), :]
    for p in range(4):
        b = where[0, 0, p]
        rhs[b] = rhs[b] + rate[0, 0, p] * row_of(row[well[0, 0, p]], (rows0, rows1, rows2, rows3))

    def store(b, conc):
        x_next[b] = conc.astype(BF16)

    upstream = from_grid(neighbour, grid)
    for r in range(0, 8, 2):
        for ahead in (r + 2, r + 3):
            if ahead < 8:
                start(ahead)
        for copy in copies[r] + copies[r + 1]:
            copy.wait()
        sweep(range(8 * r, 8 * r + 16), upstream, rhs, upwind, diag, store)
    send_edges(lambda b: x_next[b], to_near, to_far, to_mate, to_other)


def fill(grid, parts):
    if len(parts) == 1:
        for b in range(64):
            grid[at(b)] = parts[0][b]
    else:
        interior, edges, corners = parts
        for b in INTERIOR:
            grid[at(b)] = interior[b]
        for b in EDGES:
            grid[at(b)] = edges[b]
        for i, b in enumerate(CORNERS):
            grid[at(b)] = corners[i]


def inner(count, dtype, neighbour, *refs):
    parts, (rhs, upwind, diag, interior, grid) = refs[:count], refs[count:]
    fill(grid, parts)

    def store(b, conc):
        interior[b] = conc.astype(dtype)

    upstream = from_grid(neighbour, grid)
    for i in range(0, 36, 18):
        sweep(INTERIOR[i : i + 18], upstream, rhs, upwind, diag, store)


def middle(neighbour, local, near, far, mate, other, rhs, upwind, diag, edges, grid):
    for b in range(64):
        grid[at(b)] = local[at(b)]
    widen(grid, near, far, mate, other)

    def store(b, conc):
        edges[b] = conc.astype(BF16)

    sweep(EDGES, from_grid(neighbour, grid), rhs, upwind, diag, store)


def sweep_corners(neighbour, grid, mate, other, rhs, upwind, diag, store):
    even, above, below = even_tile(), above_is_real(), below_is_real()
    halos = [only_if(above, jnp.where(even, other[i], mate[i])) for i in range(2)]
    halos += [only_if(below, jnp.where(even, mate[i], other[i])) for i in range(2)]

    def upstream(b):
        i = CORNERS.index(b)
        slots = [neighbour[3 * b + k] for k in range(3)]
        return jnp.concatenate([jnp.where(n == CORNER_HALOS[i], halos[i], grid[n]) for n in slots], axis=1)

    sweep(CORNERS, upstream, rhs, upwind, diag, store)


def outer(neighbour, edges, grid, mate, other, rhs, upwind, diag, corners, to_near, to_far, to_mate, to_other):
    def store(b, conc):
        corners[CORNERS.index(b)] = conc.astype(BF16)

    sweep_corners(neighbour, grid, mate, other, rhs, upwind, diag, store)
    block = lambda b: corners[CORNERS.index(b)] if b in CORNERS else edges[b]
    send_edges(block, to_near, to_far, to_mate, to_other)


def middle_last(
    neighbour, local, interior, near, far, mate, other, rhs, upwind, diag, out, ends, grid, held, sems
):
    for b in range(64):
        grid[at(b)] = local[at(b)]
    widen(grid, near, far, mate, other)
    rows = held.reshape(32 * 64, 128)

    def store(b, conc):
        rows[pl.ds(b, 32, stride=64), :] = conc

    sweep(EDGES, from_grid(neighbour, grid), rhs, upwind, diag, store)
    for b in INTERIOR:
        store(b, interior[b])
    copies = []
    for r in range(1, 7):
        part = pl.ds(8 * r, 8)
        copies.append(pltpu.make_async_copy(held.at[:, part], out.at[:, part], sems.at[r]))
        copies[-1].start()
    for i, r in enumerate((0, 7)):
        ends[:, pl.ds(8 * i, 8)] = held[:, pl.ds(8 * r, 8)]
    for copy in copies:
        copy.wait()


def outer_last(neighbour, partial, grid, mate, other, rhs, upwind, diag, ends, out, held, sems):
    del partial
    held[...] = ends[...]
    rows = held.reshape(32 * 16, 128)

    def store(b, conc):
        rows[pl.ds(b if b < 8 else b - 48, 32, stride=16), :] = conc

    sweep_corners(neighbour, grid, mate, other, rhs, upwind, diag, store)
    copies = []
    for i, r in enumerate((0, 7)):
        copies.append(pltpu.make_async_copy(held.at[:, pl.ds(8 * i, 8)], out.at[:, pl.ds(8 * r, 8)], sems.at[i]))
        copies[-1].start()
    for copy in copies:
        copy.wait()


VMEM, SMEM, ANY, HBM = (pl.BlockSpec(memory_space=m) for m in (pltpu.VMEM, pltpu.SMEM, pl.ANY, pltpu.HBM))

SMEM_FROM_HBM = "scalars"


def call(kernel, outs, args, scratch=(), aliases=None, flops=0, moved=0):
    values = []
    for where, value in args:
        if where is VMEM:
            value = pltpu.with_memory_space_constraint(value, pltpu.VMEM)
        if where in (HBM, SMEM_FROM_HBM):
            value = pltpu.with_memory_space_constraint(value, pltpu.HBM)
        values.append(value)
    shapes = [pltpu.VMEM(s.shape, s.dtype) if where is VMEM else s for where, s in outs]
    return pl.pallas_call(
        kernel,
        out_shape=shapes,
        in_specs=[SMEM if where is SMEM_FROM_HBM else where for where, _ in args],
        out_specs=[where for where, _ in outs],
        scratch_shapes=list(scratch),
        input_output_aliases=aliases or {},
        cost_estimate=pl.CostEstimate(flops=flops, bytes_accessed=moved, transcendentals=0),
        compiler_params=pltpu.CompilerParams(vmem_limit_bytes=6 * 2**20),
    )(*values)


def blocks(count, dtype=BF16):
    return VMEM, jax.ShapeDtypeStruct((count, 32, 128), dtype)


def body(
    old_conc, upwind, diag_inverse, neighbours, streams, injector_row, perf_well, perf_block, perf_rate
):
    tiles, slabs = lax.axis_size("tile"), lax.axis_size("slab")
    both = ("tile", "slab")
    on_chip = [(s, s ^ 1) for s in range(slabs)]
    far_pairs, mates, others = [], [], []
    for t in range(tiles):
        for s in range(slabs):
            here = t * slabs + s
            far_pairs.append((here, t * slabs + 3 - s if s in (1, 2) else (t ^ 1) * slabs + s))
            mates.append((here, (t ^ 1) * slabs + s))
            other = t - 1 if t % 2 == 0 else t + 1
            others.append((here, other * slabs + s if 0 <= other < tiles else t * slabs + (s ^ 1)))

    def vmem(*values):
        return [(VMEM, v) for v in values]

    def exchange(to_near, to_far, to_mate, to_other):
        from_far = lax.ppermute(to_far, both, far_pairs)
        from_near = lax.ppermute(to_near, "slab", on_chip)
        from_mate = lax.ppermute(to_mate, both, mates)
        from_other = lax.ppermute(to_other, both, others)
        return from_near, from_far, from_mate, from_other

    def exchange_corners(from_near, from_far):
        to_mate, to_other = call(pass_corners, [blocks(2)] * 2, vmem(from_near, from_far))
        return lax.ppermute(to_mate, both, mates), lax.ppermute(to_other, both, others)

    dma = pltpu.SemaphoreType.DMA
    held = pltpu.VMEM((32, 64, 128), F32)
    grid = pltpu.VMEM((100, 32, 128), BF16)
    edges = [blocks(8)] * 4
    neighbour = (SMEM, neighbours.reshape(-1))
    old = (HBM, old_conc.reshape(32, 64, 128))
    work = dict(flops=2 * 64 * 4 * 32 * 128 * 128, moved=9 * 2**20)

    (everyone,) = call(spread, [blocks(PLANE)], [(HBM, streams)], [pltpu.VMEM((1, 32, 128), F32), dma(())])
    planes = [list(range(z, z + PLANE)) for z in range(0, tiles, PLANE)]
    rows = [lax.all_to_all(everyone, "tile", 0, 0, axis_index_groups=planes)]
    for m in (1, 2, 3):
        rows.append(lax.ppermute(rows[0], "tile", [(t, t ^ (m * PLANE)) for t in range(tiles)]))

    x, to_near, to_far = call(
        prepare, [blocks(64), blocks(8), blocks(8)], [old], [held, dma((8,))], moved=4 * 2**20
    )
    from_far = lax.ppermute(to_far, both, far_pairs)
    from_near = lax.ppermute(to_near, "slab", on_chip)
    to_mate, to_other = call(rows_to_send, [blocks(WIDE)] * 2, vmem(x, from_near, from_far))
    got = from_near, from_far, lax.ppermute(to_mate, both, mates), lax.ppermute(to_other, both, others)

    upwind_shape = jax.ShapeDtypeStruct((64, 3, 128, 128), BF16)
    diag_shape = jax.ShapeDtypeStruct((64, 128, 128), BF16)
    wells = [(SMEM_FROM_HBM, v) for v in (perf_well, injector_row, perf_block, perf_rate)]
    x, rhs, *rest = call(
        sweep_first,
        [blocks(64), blocks(64, F32), (VMEM, upwind_shape), (VMEM, diag_shape), *edges],
        [neighbour, *wells, *vmem(x, *got, *rows), old]
        + [(HBM, upwind.reshape(upwind_shape.shape)), (HBM, diag_inverse.reshape(diag_shape.shape))],
        [grid, held, dma((8,)), dma((16,))],
        **work,
    )
    weights, sent = rest[:2], rest[2:]
    parts = [x]
    for last in (False, True):
        got = exchange(*sent)
        interior, local = call(
            functools.partial(inner, len(parts), F32 if last else BF16),
            [blocks(64, F32 if last else BF16), blocks(100)],
            [neighbour, *vmem(*parts, rhs, *weights)],
            **work,
        )
        ends = exchange_corners(*got[:2])
        if last:
            break
        edge_blocks, whole_grid = call(
            middle, [blocks(64), blocks(100)], [neighbour, *vmem(local, *got, rhs, *weights)], **work
        )
        corners, *sent = call(
            outer, [blocks(4), *edges], [neighbour, *vmem(edge_blocks, whole_grid, *ends, rhs, *weights)]
        )
        parts = [interior, edge_blocks, corners]
    whole = (ANY, jax.ShapeDtypeStruct((32, 64, 128), F32))
    partial, border, whole_grid = call(
        middle_last,
        [whole, (VMEM, jax.ShapeDtypeStruct((32, 16, 128), F32)), blocks(100)],
        [neighbour, *vmem(local, interior, *got, rhs, *weights)],
        [held, dma((8,))],
        **work,
    )
    (out,) = call(
        outer_last,
        [whole],
        [neighbour, (ANY, partial), *vmem(whole_grid, *ends, rhs, *weights, border)],
        [pltpu.VMEM((32, 16, 128), F32), pltpu.SemaphoreType.DMA((2,))],
        {1: 0},
    )
    return out.reshape(old_conc.shape)


def solution(mesh):
    in_specs = (
        P(None, "tile", "slab", None),
        P("tile", "slab", None, None, None),
        P("tile", "slab", None, None),
        P("tile", "slab", None),
        P("tile", None, None),
        P(),
        P("tile", "slab", None),
        P("tile", "slab", None),
        P("tile", "slab", None),
    )
    out_specs = P(None, "tile", "slab", None)
    return jax.shard_map(body, mesh=mesh, in_specs=in_specs, out_specs=out_specs, check_vma=False)
```

```python
import functools

import jax
import jax.numpy as jnp
from jax import lax
from jax.experimental import pallas as pl
from jax.experimental.pallas import tpu as pltpu
from jax.sharding import PartitionSpec as P

BF16 = jnp.bfloat16
F32 = jnp.float32
WIDE = 10
CORNERS = (0, 7, 56, 63)
CORNER_HALOS = (0, 9, 90, 99)
INTERIOR = tuple(b for b in range(64) if 0 < b // 8 < 7 and 0 < b % 8 < 7)
EDGES = tuple(b for b in range(64) if b not in INTERIOR and b not in CORNERS)

dot_t = functools.partial(
    lax.dot_general,
    dimension_numbers=(((1,), (1,)), ((), ())),
    preferred_element_type=F32,
)


def parity():
    return lax.rem(lax.axis_index("slab"), 2)


def even_tile():
    return lax.rem(lax.axis_index("tile"), 2) == 0


def far_is_real():
    slab = lax.axis_index("slab")
    return jnp.logical_or(slab == 1, slab == 2)


def above_is_real():
    return lax.axis_index("tile") > 0


def below_is_real():
    return lax.axis_index("tile") < lax.axis_size("tile") - 1


def only_if(real, value):
    return jnp.where(real, value, jnp.zeros_like(value))


def send_edges(x, to_near, to_far, to_mate, to_other):
    right, even = parity() == 0, even_tile()
    for r in range(8):
        first, last = x(r * 8), x(r * 8 + 7)
        to_near[r] = jnp.where(right, last, first)
        to_far[r] = jnp.where(right, first, last)
        top, bottom = x(r), x(56 + r)
        to_mate[r] = jnp.where(even, bottom, top)
        to_other[r] = jnp.where(even, top, bottom)


def bring_old(old, held, sems):
    copies = []
    for r in range(8):
        part = pl.ds(8 * r, 8)
        copies.append(pltpu.make_async_copy(old.at[:, part], held.at[:, part], sems.at[r]))
        copies[-1].start()
    return copies


def spread(stream, row, held, sem):
    copy = pltpu.make_async_copy(stream, held, sem)
    copy.start()
    copy.wait()
    row[...] = held[...].astype(BF16)


def join(part0, part1, part2, part3, whole):
    count = part0.shape[0]
    for m, part in enumerate((part0, part1, part2, part3)):
        whole[pl.ds(m * count, count)] = part[...]


def prepare(old, x, to_near, to_far, held, sems):
    copies = bring_old(old, held, sems)
    rows = held.reshape(32 * 64, 128)
    right = parity() == 0
    for r in range(8):
        copies[r].wait()
        for b in range(8 * r, 8 * r + 8):
            x[b] = rows[pl.ds(b, 32, stride=64), :].astype(BF16)
        first, last = x[8 * r], x[8 * r + 7]
        to_near[r] = jnp.where(right, last, first)
        to_far[r] = jnp.where(right, first, last)


def rows_to_send(x, from_near, from_far, to_mate, to_other):
    right, even = parity() == 0, even_tile()
    real = far_is_real()
    rows = []
    for r in (0, 7):
        near, far = from_near[r], only_if(real, from_far[r])
        rows.append([jnp.where(right, far, near), *(x[8 * r + c] for c in range(8)), jnp.where(right, near, far)])
    for i in range(WIDE):
        top, bottom = rows[0][i], rows[1][i]
        to_mate[i] = jnp.where(even, bottom, top)
        to_other[i] = jnp.where(even, top, bottom)


def pass_corners(from_near, from_far, to_mate, to_other):
    right, even = parity() == 0, even_tile()
    real = far_is_real()
    ends = []
    for r in (0, 7):
        near, far = from_near[r], only_if(real, from_far[r])
        ends.append((jnp.where(right, far, near), jnp.where(right, near, far)))
    for i in range(2):
        top, bottom = ends[0][i], ends[1][i]
        to_mate[i] = jnp.where(even, bottom, top)
        to_other[i] = jnp.where(even, top, bottom)


def at(b):
    return (b // 8 + 1) * WIDE + b % 8 + 1


def widen(grid, from_near, from_far, from_mate, from_other):
    right, even = parity() == 0, even_tile()
    real, above, below = far_is_real(), above_is_real(), below_is_real()
    for r in range(8):
        near, far = from_near[r], only_if(real, from_far[r])
        grid[(r + 1) * WIDE] = jnp.where(right, far, near)
        grid[(r + 1) * WIDE + 9] = jnp.where(right, near, far)
    count = from_mate.shape[0]
    first = (WIDE - count) // 2
    for c in range(count):
        mate, other = from_mate[c], from_other[c]
        grid[first + c] = only_if(above, jnp.where(even, other, mate))
        grid[90 + first + c] = only_if(below, jnp.where(even, mate, other))


def sweep(ids, upstream, rhs, upwind, diag, store):
    remainders = []
    for b in ids:
        weights = jnp.concatenate([upwind[b, k] for k in range(3)], axis=1)
        remainders.append((rhs[b] - dot_t(upstream(b), weights)).astype(BF16))
    for i in range(0, len(ids), 2):
        both = jnp.concatenate(remainders[i : i + 2], axis=0)
        weights = jnp.concatenate([diag[ids[i]], diag[ids[i + 1]]], axis=0)
        conc = dot_t(both, weights)
        store(ids[i], conc[:32, :128])
        store(ids[i + 1], conc[32:, 128:])


def from_grid(neighbour, grid):
    return lambda b: jnp.concatenate([grid[neighbour[3 * b + k]] for k in range(3)], axis=1)


def row_of(well, parts):
    away = well ^ lax.axis_index("tile")
    place = (away // 4) % 4 * 4 + away // 16
    row = parts[0][place]
    for m in range(1, 4):
        row = jnp.where(away % 4 == m, parts[m][place], row)
    return row.astype(F32)


def sweep_first(
    neighbour, x, near, far, mate, other, old, upwind_far, diag_far, x_next, rhs, upwind, diag, grid, held, old_sems, sems
):
    old_copies = bring_old(old, held, old_sems)
    copies = []
    for r in range(8):
        part = pl.ds(8 * r, 8)
        copies.append(
            (
                pltpu.make_async_copy(upwind_far.at[part], upwind.at[part], sems.at[2 * r]),
                pltpu.make_async_copy(diag_far.at[part], diag.at[part], sems.at[2 * r + 1]),
            )
        )

    def start(r):
        for copy in copies[r]:
            copy.start()

    for r in range(4):
        start(r)
    widen(grid, near, far, mate, other)
    for b in range(64):
        grid[at(b)] = x[b]
    old_rows = held.reshape(32 * 64, 128)
    for r in range(8):
        old_copies[r].wait()
        for b in range(8 * r, 8 * r + 8):
            rhs[b] = old_rows[pl.ds(b, 32, stride=64), :]

    def store(b, conc):
        x_next[b] = conc.astype(BF16)

    upstream = from_grid(neighbour, grid)
    for r in range(0, 8, 2):
        for ahead in (r + 4, r + 5):
            if ahead < 8:
                start(ahead)
        for copy in copies[r] + copies[r + 1]:
            copy.wait()
        sweep(range(8 * r, 8 * r + 16), upstream, rhs, upwind, diag, store)


def inject(
    neighbour, well, row, where, rate, rows0, rows1, rows2, rows3, x_in, rhs_in, grid, upwind, diag,
    x, rhs, to_near, to_far, to_mate, to_other,
):
    x[...] = x_in[...]
    rhs[...] = rhs_in[...]
    for p in range(4):
        b = where[0, 0, p]
        rhs[b] = rhs[b] + rate[0, 0, p] * row_of(row[well[0, 0, p]], (rows0, rows1, rows2, rows3))

    def store(b, conc):
        x[b] = conc.astype(BF16)

    sweep([where[0, 0, p] for p in range(4)], from_grid(neighbour, grid), rhs, upwind, diag, store)
    send_edges(lambda b: x[b], to_near, to_far, to_mate, to_other)


def fill(grid, parts):
    if len(parts) == 1:
        for b in range(64):
            grid[at(b)] = parts[0][b]
    else:
        interior, edges, corners = parts
        for b in INTERIOR:
            grid[at(b)] = interior[b]
        for b in EDGES:
            grid[at(b)] = edges[b]
        for i, b in enumerate(CORNERS):
            grid[at(b)] = corners[i]


def inner(count, dtype, neighbour, *refs):
    parts, (rhs, upwind, diag, interior, grid) = refs[:count], refs[count:]
    fill(grid, parts)

    def store(b, conc):
        interior[b] = conc.astype(dtype)

    upstream = from_grid(neighbour, grid)
    for i in range(0, 36, 18):
        sweep(INTERIOR[i : i + 18], upstream, rhs, upwind, diag, store)


def middle(neighbour, local, near, far, mate, other, rhs, upwind, diag, edges, grid):
    for b in range(64):
        grid[at(b)] = local[at(b)]
    widen(grid, near, far, mate, other)

    def store(b, conc):
        edges[b] = conc.astype(BF16)

    sweep(EDGES, from_grid(neighbour, grid), rhs, upwind, diag, store)


def sweep_corners(neighbour, grid, mate, other, rhs, upwind, diag, store):
    even, above, below = even_tile(), above_is_real(), below_is_real()
    halos = [only_if(above, jnp.where(even, other[i], mate[i])) for i in range(2)]
    halos += [only_if(below, jnp.where(even, mate[i], other[i])) for i in range(2)]

    def upstream(b):
        i = CORNERS.index(b)
        slots = [neighbour[3 * b + k] for k in range(3)]
        return jnp.concatenate([jnp.where(n == CORNER_HALOS[i], halos[i], grid[n]) for n in slots], axis=1)

    sweep(CORNERS, upstream, rhs, upwind, diag, store)


def outer(neighbour, edges, grid, mate, other, rhs, upwind, diag, corners, to_near, to_far, to_mate, to_other):
    def store(b, conc):
        corners[CORNERS.index(b)] = conc.astype(BF16)

    sweep_corners(neighbour, grid, mate, other, rhs, upwind, diag, store)
    block = lambda b: corners[CORNERS.index(b)] if b in CORNERS else edges[b]
    send_edges(block, to_near, to_far, to_mate, to_other)


def middle_last(neighbour, local, interior, near, far, mate, other, rhs, upwind, diag, out, grid, held, sems):
    copies = []

    def send(block, b):
        copies.append(pltpu.make_async_copy(block, out.at[:, b], sems.at[b]))
        copies[-1].start()

    for b in INTERIOR:
        send(interior.at[b], b)
    for b in range(64):
        grid[at(b)] = local[at(b)]
    widen(grid, near, far, mate, other)

    def store(b, conc):
        held[EDGES.index(b)] = conc

    sweep(EDGES, from_grid(neighbour, grid), rhs, upwind, diag, store)
    for i, b in enumerate(EDGES):
        send(held.at[i], b)
    for copy in copies:
        copy.wait()


def outer_last(neighbour, partial, grid, mate, other, rhs, upwind, diag, out, held, sems):
    del partial

    def store(b, conc):
        held[CORNERS.index(b)] = conc

    sweep_corners(neighbour, grid, mate, other, rhs, upwind, diag, store)
    copies = [pltpu.make_async_copy(held.at[i], out.at[:, b], sems.at[i]) for i, b in enumerate(CORNERS)]
    for copy in copies:
        copy.start()
    for copy in copies:
        copy.wait()


VMEM, SMEM, ANY, HBM = (pl.BlockSpec(memory_space=m) for m in (pltpu.VMEM, pltpu.SMEM, pl.ANY, pltpu.HBM))

SMEM_FROM_HBM = "scalars"


def call(kernel, outs, args, scratch=(), aliases=None, flops=0, moved=0):
    values = []
    for where, value in args:
        if where is VMEM:
            value = pltpu.with_memory_space_constraint(value, pltpu.VMEM)
        if where in (HBM, SMEM_FROM_HBM):
            value = pltpu.with_memory_space_constraint(value, pltpu.HBM)
        values.append(value)
    shapes = []
    for where, s in outs:
        if where is VMEM:
            s = pltpu.VMEM(s.shape, s.dtype)
        if where is HBM:
            s = pltpu.HBM(s.shape, s.dtype)
        shapes.append(s)
    return pl.pallas_call(
        kernel,
        out_shape=shapes,
        in_specs=[SMEM if where is SMEM_FROM_HBM else where for where, _ in args],
        out_specs=[where for where, _ in outs],
        scratch_shapes=list(scratch),
        input_output_aliases=aliases or {},
        cost_estimate=pl.CostEstimate(flops=flops, bytes_accessed=moved, transcendentals=0),
        compiler_params=pltpu.CompilerParams(vmem_limit_bytes=6 * 2**20),
    )(*values)


def blocks(count, dtype=BF16):
    return VMEM, jax.ShapeDtypeStruct((count, 32, 128), dtype)


def body(
    old_conc, upwind, diag_inverse, neighbours, streams, injector_row, perf_well, perf_block, perf_rate
):
    tiles, slabs = lax.axis_size("tile"), lax.axis_size("slab")
    both = ("tile", "slab")
    on_chip = [(s, s ^ 1) for s in range(slabs)]
    far_pairs, mates, others = [], [], []
    for t in range(tiles):
        for s in range(slabs):
            here = t * slabs + s
            far_pairs.append((here, t * slabs + 3 - s if s in (1, 2) else (t ^ 1) * slabs + s))
            mates.append((here, (t ^ 1) * slabs + s))
            other = t - 1 if t % 2 == 0 else t + 1
            others.append((here, other * slabs + s if 0 <= other < tiles else t * slabs + (s ^ 1)))

    def vmem(*values):
        return [(VMEM, v) for v in values]

    def exchange(to_near, to_far, to_mate, to_other):
        from_far = lax.ppermute(to_far, both, far_pairs)
        from_near = lax.ppermute(to_near, "slab", on_chip)
        from_mate = lax.ppermute(to_mate, both, mates)
        from_other = lax.ppermute(to_other, both, others)
        return from_near, from_far, from_mate, from_other

    def exchange_corners(from_near, from_far):
        to_mate, to_other = call(pass_corners, [blocks(2)] * 2, vmem(from_near, from_far))
        return lax.ppermute(to_mate, both, mates), lax.ppermute(to_other, both, others)

    dma = pltpu.SemaphoreType.DMA
    held = pltpu.VMEM((32, 64, 128), F32)
    grid = pltpu.VMEM((100, 32, 128), BF16)
    edges = [blocks(8)] * 4
    neighbour = (SMEM, neighbours.reshape(-1))
    old = (HBM, old_conc.reshape(32, 64, 128))
    work = dict(flops=2 * 64 * 4 * 32 * 128 * 128, moved=9 * 2**20)

    def swaps(part, step):
        return [part] + [lax.ppermute(part, "tile", [(t, t ^ (m * step)) for t in range(tiles)]) for m in (1, 2, 3)]

    (part,) = call(spread, [blocks(1)], [(HBM, streams)], [pltpu.VMEM((1, 32, 128), F32), dma(())])
    for step in (16, 4):
        (part,) = call(join, [blocks(4 * part.shape[0])], vmem(*swaps(part, step)))
    rows = swaps(part, 1)

    x, to_near, to_far = call(
        prepare, [blocks(64), blocks(8), blocks(8)], [old], [held, dma((8,))], moved=4 * 2**20
    )
    from_far = lax.ppermute(to_far, both, far_pairs)
    from_near = lax.ppermute(to_near, "slab", on_chip)
    to_mate, to_other = call(rows_to_send, [blocks(WIDE)] * 2, vmem(x, from_near, from_far))
    got = from_near, from_far, lax.ppermute(to_mate, both, mates), lax.ppermute(to_other, both, others)

    upwind_shape = jax.ShapeDtypeStruct((64, 3, 128, 128), BF16)
    diag_shape = jax.ShapeDtypeStruct((64, 128, 128), BF16)
    wells = [(SMEM_FROM_HBM, v) for v in (perf_well, injector_row, perf_block, perf_rate)]
    x, rhs, *weights, whole_grid = call(
        sweep_first,
        [blocks(64), blocks(64, F32), (VMEM, upwind_shape), (VMEM, diag_shape), blocks(100)],
        [neighbour, *vmem(x, *got), old]
        + [(HBM, upwind.reshape(upwind_shape.shape)), (HBM, diag_inverse.reshape(diag_shape.shape))],
        [held, dma((8,)), dma((16,))],
        **work,
    )
    x, rhs, *sent = call(
        inject,
        [blocks(64), blocks(64, F32), *edges],
        [neighbour, *wells, *vmem(*rows, x, rhs, whole_grid, *weights)],
    )
    parts = [x]
    for last in (False, True):
        got = exchange(*sent)
        interior, local = call(
            functools.partial(inner, len(parts), F32 if last else BF16),
            [blocks(64, F32 if last else BF16), blocks(100)],
            [neighbour, *vmem(*parts, rhs, *weights)],
            **work,
        )
        ends = exchange_corners(*got[:2])
        if last:
            break
        edge_blocks, whole_grid = call(
            middle, [blocks(64), blocks(100)], [neighbour, *vmem(local, *got, rhs, *weights)], **work
        )
        corners, *sent = call(
            outer, [blocks(4), *edges], [neighbour, *vmem(edge_blocks, whole_grid, *ends, rhs, *weights)]
        )
        parts = [interior, edge_blocks, corners]
    whole = (ANY, jax.ShapeDtypeStruct((32, 64, 128), F32))
    partial, whole_grid = call(
        middle_last,
        [whole, blocks(100)],
        [neighbour, *vmem(local, interior, *got, rhs, *weights)],
        [pltpu.VMEM((24, 32, 128), F32), dma((64,))],
        **work,
    )
    (out,) = call(
        outer_last,
        [whole],
        [neighbour, (ANY, partial), *vmem(whole_grid, *ends, rhs, *weights)],
        [pltpu.VMEM((4, 32, 128), F32), dma((4,))],
        {1: 0},
    )
    return out.reshape(old_conc.shape)


def solution(mesh):
    in_specs = (
        P(None, "tile", "slab", None),
        P("tile", "slab", None, None, None),
        P("tile", "slab", None, None),
        P("tile", "slab", None),
        P("tile", None, None),
        P(),
        P("tile", "slab", None),
        P("tile", "slab", None),
        P("tile", "slab", None),
    )
    out_specs = P(None, "tile", "slab", None)
    return jax.shard_map(body, mesh=mesh, in_specs=in_specs, out_specs=out_specs, check_vma=False)
```

```python
import functools

import jax
import jax.numpy as jnp
from jax import lax
from jax.experimental import pallas as pl
from jax.experimental.pallas import tpu as pltpu
from jax.sharding import PartitionSpec as P

BF16 = jnp.bfloat16
F32 = jnp.float32
WIDE = 10
CORNERS = (0, 7, 56, 63)
CORNER_HALOS = (0, 9, 90, 99)
INNER = tuple(b for b in range(64) if b not in CORNERS)

dot_t = functools.partial(
    lax.dot_general,
    dimension_numbers=(((1,), (1,)), ((), ())),
    preferred_element_type=F32,
)


def parity():
    return lax.rem(lax.axis_index("slab"), 2)


def even_tile():
    return lax.rem(lax.axis_index("tile"), 2) == 0


def far_is_real():
    slab = lax.axis_index("slab")
    return jnp.logical_or(slab == 1, slab == 2)


def above_is_real():
    return lax.axis_index("tile") > 0


def below_is_real():
    return lax.axis_index("tile") < lax.axis_size("tile") - 1


def only_if(real, value):
    return jnp.where(real, value, jnp.zeros_like(value))


def send_edges(x, to_near, to_far, to_mate, to_other):
    right, even = parity() == 0, even_tile()
    for r in range(8):
        first, last = x(r * 8), x(r * 8 + 7)
        to_near[r] = jnp.where(right, last, first)
        to_far[r] = jnp.where(right, first, last)
        top, bottom = x(r), x(56 + r)
        to_mate[r] = jnp.where(even, bottom, top)
        to_other[r] = jnp.where(even, top, bottom)


def bring_old(old, held, sems):
    copies = []
    for r in range(8):
        part = pl.ds(8 * r, 8)
        copies.append(pltpu.make_async_copy(old.at[:, part], held.at[:, part], sems.at[r]))
        copies[-1].start()
    return copies


def join(part0, part1, part2, part3, *after_and_whole):
    count, whole = part0.shape[0], after_and_whole[-1]
    for m, part in enumerate((part0, part1, part2, part3)):
        whole[pl.ds(m * count, count)] = part[...]


def prepare(old, stream, x, rhs, to_near, to_far, row, held, held_row, sems):
    copies = bring_old(old, held, sems)
    row_copy = pltpu.make_async_copy(stream, held_row, sems.at[8])
    row_copy.start()
    rows = held.reshape(32 * 64, 128)
    right = parity() == 0
    for r in range(8):
        copies[r].wait()
        for b in range(8 * r, 8 * r + 8):
            block = rows[pl.ds(b, 32, stride=64), :]
            rhs[b] = block
            x[b] = block.astype(BF16)
        first, last = x[8 * r], x[8 * r + 7]
        to_near[r] = jnp.where(right, last, first)
        to_far[r] = jnp.where(right, first, last)
    row_copy.wait()
    row[...] = held_row[...].astype(BF16)


def rows_to_send(x, from_near, from_far, to_mate, to_other):
    right, even = parity() == 0, even_tile()
    real = far_is_real()
    rows = []
    for r in (0, 7):
        near, far = from_near[r], only_if(real, from_far[r])
        rows.append([jnp.where(right, far, near), *(x[8 * r + c] for c in range(8)), jnp.where(right, near, far)])
    for i in range(WIDE):
        top, bottom = rows[0][i], rows[1][i]
        to_mate[i] = jnp.where(even, bottom, top)
        to_other[i] = jnp.where(even, top, bottom)


def pass_corners(from_near, from_far, to_mate, to_other):
    right, even = parity() == 0, even_tile()
    real = far_is_real()
    ends = []
    for r in (0, 7):
        near, far = from_near[r], only_if(real, from_far[r])
        ends.append((jnp.where(right, far, near), jnp.where(right, near, far)))
    for i in range(2):
        top, bottom = ends[0][i], ends[1][i]
        to_mate[i] = jnp.where(even, bottom, top)
        to_other[i] = jnp.where(even, top, bottom)


def at(b):
    return (b // 8 + 1) * WIDE + b % 8 + 1


def widen(grid, from_near, from_far, from_mate, from_other):
    right, even = parity() == 0, even_tile()
    real, above, below = far_is_real(), above_is_real(), below_is_real()
    for r in range(8):
        near, far = from_near[r], only_if(real, from_far[r])
        grid[(r + 1) * WIDE] = jnp.where(right, far, near)
        grid[(r + 1) * WIDE + 9] = jnp.where(right, near, far)
    count = from_mate.shape[0]
    first = (WIDE - count) // 2
    for c in range(count):
        mate, other = from_mate[c], from_other[c]
        grid[first + c] = only_if(above, jnp.where(even, other, mate))
        grid[90 + first + c] = only_if(below, jnp.where(even, mate, other))


def sweep(ids, upstream, rhs, upwind, diag, store):
    remainders = []
    for b in ids:
        weights = jnp.concatenate([upwind[b, k] for k in range(3)], axis=1)
        remainders.append((rhs[b] - dot_t(upstream(b), weights)).astype(BF16))
    for i in range(0, len(ids), 2):
        both = jnp.concatenate(remainders[i : i + 2], axis=0)
        weights = jnp.concatenate([diag[ids[i]], diag[ids[i + 1]]], axis=0)
        conc = dot_t(both, weights)
        store(ids[i], conc[:32, :128])
        store(ids[i + 1], conc[32:, 128:])


def from_grid(neighbour, grid):
    return lambda b: jnp.concatenate([grid[neighbour[3 * b + k]] for k in range(3)], axis=1)


def row_of(well, parts):
    away = well ^ lax.axis_index("tile")
    place = (away // 4) % 4 * 4 + away // 16
    row = parts[0][place]
    for m in range(1, 4):
        row = jnp.where(away % 4 == m, parts[m][place], row)
    return row.astype(F32)


def load(after, upwind_far, diag_far, upwind, diag, sems):
    del after
    copies = [
        pltpu.make_async_copy(upwind_far, upwind, sems.at[0]),
        pltpu.make_async_copy(diag_far, diag, sems.at[1]),
    ]
    for copy in copies:
        copy.start()
    for copy in copies:
        copy.wait()


def sweep_first(neighbour, x, near, far, mate, other, rhs, upwind, diag, x_next, grid):
    fill(grid, x, ())
    widen(grid, near, far, mate, other)

    def store(b, conc):
        x_next[b] = conc.astype(BF16)

    upstream = from_grid(neighbour, grid)
    for i in range(0, 64, 16):
        sweep(range(i, i + 16), upstream, rhs, upwind, diag, store)


def inject(
    neighbour, well, row, where, rate, rows0, rows1, rows2, rows3, x_in, rhs_in, grid, upwind, diag,
    x, rhs, to_near, to_far, to_mate, to_other,
):
    x[...] = x_in[...]
    rhs[...] = rhs_in[...]
    for p in range(4):
        b = where[0, 0, p]
        rhs[b] = rhs[b] + rate[0, 0, p] * row_of(row[well[0, 0, p]], (rows0, rows1, rows2, rows3))

    def store(b, conc):
        x[b] = conc.astype(BF16)

    sweep([where[0, 0, p] for p in range(4)], from_grid(neighbour, grid), rhs, upwind, diag, store)
    send_edges(lambda b: x[b], to_near, to_far, to_mate, to_other)


def fill(grid, x, corners):
    for b in range(64):
        if corners and b in CORNERS:
            grid[at(b)] = corners[0][CORNERS.index(b)]
        else:
            grid[at(b)] = x[b]


def middle(count, neighbour, x, *refs):
    corners, (near, far, mate, other, rhs, upwind, diag, x_next, grid) = refs[:count], refs[count:]
    fill(grid, x, corners)
    widen(grid, near, far, mate, other)

    def store(b, conc):
        x_next[b] = conc.astype(BF16)

    upstream = from_grid(neighbour, grid)
    for i in range(0, 60, 20):
        sweep(INNER[i : i + 20], upstream, rhs, upwind, diag, store)


def sweep_corners(neighbour, grid, mate, other, rhs, upwind, diag, store):
    even, above, below = even_tile(), above_is_real(), below_is_real()
    halos = [only_if(above, jnp.where(even, other[i], mate[i])) for i in range(2)]
    halos += [only_if(below, jnp.where(even, mate[i], other[i])) for i in range(2)]

    def upstream(b):
        i = CORNERS.index(b)
        slots = [neighbour[3 * b + k] for k in range(3)]
        return jnp.concatenate([jnp.where(n == CORNER_HALOS[i], halos[i], grid[n]) for n in slots], axis=1)

    sweep(CORNERS, upstream, rhs, upwind, diag, store)


def outer(neighbour, edges, grid, mate, other, rhs, upwind, diag, corners, to_near, to_far, to_mate, to_other):
    def store(b, conc):
        corners[CORNERS.index(b)] = conc.astype(BF16)

    sweep_corners(neighbour, grid, mate, other, rhs, upwind, diag, store)
    block = lambda b: corners[CORNERS.index(b)] if b in CORNERS else edges[b]
    send_edges(block, to_near, to_far, to_mate, to_other)


def middle_last(neighbour, x, corners, near, far, mate, other, rhs, upwind, diag, out, grid, held, sems):
    fill(grid, x, [corners])
    widen(grid, near, far, mate, other)
    copies = []

    def store(b, conc):
        held[b] = conc

    upstream = from_grid(neighbour, grid)
    for ids in (INNER[:24], INNER[24:48], INNER[48:]):
        sweep(ids, upstream, rhs, upwind, diag, store)
        for b in ids:
            copies.append(pltpu.make_async_copy(held.at[b], out.at[:, b], sems.at[b]))
            copies[-1].start()
    for copy in copies:
        copy.wait()


def outer_last(neighbour, partial, grid, mate, other, rhs, upwind, diag, out, held, sems):
    del partial

    def store(b, conc):
        held[CORNERS.index(b)] = conc

    sweep_corners(neighbour, grid, mate, other, rhs, upwind, diag, store)
    copies = [pltpu.make_async_copy(held.at[i], out.at[:, b], sems.at[i]) for i, b in enumerate(CORNERS)]
    for copy in copies:
        copy.start()
    for copy in copies:
        copy.wait()


VMEM, SMEM, ANY, HBM = (pl.BlockSpec(memory_space=m) for m in (pltpu.VMEM, pltpu.SMEM, pl.ANY, pltpu.HBM))

SMEM_FROM_HBM = "scalars"


def call(kernel, outs, args, scratch=(), aliases=None, flops=0, moved=0):
    values = []
    for where, value in args:
        if where is VMEM:
            value = pltpu.with_memory_space_constraint(value, pltpu.VMEM)
        if where in (HBM, SMEM_FROM_HBM):
            value = pltpu.with_memory_space_constraint(value, pltpu.HBM)
        values.append(value)
    shapes = []
    for where, s in outs:
        if where is VMEM:
            s = pltpu.VMEM(s.shape, s.dtype)
        if where is HBM:
            s = pltpu.HBM(s.shape, s.dtype)
        shapes.append(s)
    return pl.pallas_call(
        kernel,
        out_shape=shapes,
        in_specs=[SMEM if where is SMEM_FROM_HBM else where for where, _ in args],
        out_specs=[where for where, _ in outs],
        scratch_shapes=list(scratch),
        input_output_aliases=aliases or {},
        cost_estimate=pl.CostEstimate(flops=flops, bytes_accessed=moved, transcendentals=0),
        compiler_params=pltpu.CompilerParams(vmem_limit_bytes=6 * 2**20),
    )(*values)


def blocks(count, dtype=BF16):
    return VMEM, jax.ShapeDtypeStruct((count, 32, 128), dtype)


def body(
    old_conc, upwind, diag_inverse, neighbours, streams, injector_row, perf_well, perf_block, perf_rate
):
    tiles, slabs = lax.axis_size("tile"), lax.axis_size("slab")
    both = ("tile", "slab")
    on_chip = [(s, s ^ 1) for s in range(slabs)]
    far_pairs, mates, others = [], [], []
    for t in range(tiles):
        for s in range(slabs):
            here = t * slabs + s
            far_pairs.append((here, t * slabs + 3 - s if s in (1, 2) else (t ^ 1) * slabs + s))
            mates.append((here, (t ^ 1) * slabs + s))
            other = t - 1 if t % 2 == 0 else t + 1
            others.append((here, other * slabs + s if 0 <= other < tiles else t * slabs + (s ^ 1)))

    def vmem(*values):
        return [(VMEM, v) for v in values]

    def exchange(to_near, to_far, to_mate, to_other):
        from_far = lax.ppermute(to_far, both, far_pairs)
        from_near = lax.ppermute(to_near, "slab", on_chip)
        from_mate = lax.ppermute(to_mate, both, mates)
        from_other = lax.ppermute(to_other, both, others)
        return from_near, from_far, from_mate, from_other

    def exchange_corners(from_near, from_far):
        to_mate, to_other = call(pass_corners, [blocks(2)] * 2, vmem(from_near, from_far))
        return lax.ppermute(to_mate, both, mates), lax.ppermute(to_other, both, others)

    dma = pltpu.SemaphoreType.DMA
    held = pltpu.VMEM((32, 64, 128), F32)
    grid = pltpu.VMEM((100, 32, 128), BF16)
    edges = [blocks(8)] * 4
    neighbour = (SMEM, neighbours.reshape(-1))
    old = (HBM, old_conc.reshape(32, 64, 128))
    work = dict(flops=2 * 64 * 4 * 32 * 128 * 128, moved=9 * 2**20)

    def swaps(part, step):
        return [part] + [lax.ppermute(part, "tile", [(t, t ^ (m * step)) for t in range(tiles)]) for m in (1, 2, 3)]

    x, rhs, to_near, to_far, part = call(
        prepare,
        [blocks(64), blocks(64, F32), blocks(8), blocks(8), blocks(1)],
        [old, (HBM, streams)],
        [held, pltpu.VMEM((1, 32, 128), F32), dma((9,))],
        moved=4 * 2**20,
    )
    upwind_shape = jax.ShapeDtypeStruct((64, 3, 128, 128), BF16)
    diag_shape = jax.ShapeDtypeStruct((64, 128, 128), BF16)
    weights = call(
        load,
        [(VMEM, upwind_shape), (VMEM, diag_shape)],
        [neighbour, (HBM, upwind.reshape(upwind_shape.shape)), (HBM, diag_inverse.reshape(diag_shape.shape))],
        [dma((2,))],
        moved=8 * 2**20,
    )
    from_far = lax.ppermute(to_far, both, far_pairs)
    from_near = lax.ppermute(to_near, "slab", on_chip)
    to_mate, to_other = call(rows_to_send, [blocks(WIDE)] * 2, vmem(x, from_near, from_far))
    (part,) = call(join, [blocks(4)], vmem(*swaps(part, 16)))
    (part,) = call(join, [blocks(16)], vmem(*swaps(part, 4), weights[1], to_mate))
    rows = swaps(part, 1)

    got = from_near, from_far, lax.ppermute(to_mate, both, mates), lax.ppermute(to_other, both, others)

    wells = [(SMEM_FROM_HBM, v) for v in (perf_well, injector_row, perf_block, perf_rate)]
    x, whole_grid = call(
        sweep_first, [blocks(64), blocks(100)], [neighbour, *vmem(x, *got, rhs, *weights)], **work
    )
    x, rhs, *sent = call(
        inject,
        [blocks(64), blocks(64, F32), *edges],
        [neighbour, *wells, *vmem(*rows, x, rhs, whole_grid, *weights)],
    )
    corners = []
    for last in (False, True):
        got = exchange(*sent)
        ends = exchange_corners(*got[:2])
        args = [neighbour, *vmem(x, *corners, *got, rhs, *weights)]
        if last:
            break
        x, whole_grid = call(functools.partial(middle, len(corners)), [blocks(64), blocks(100)], args, **work)
        corner, *sent = call(
            outer, [blocks(4), *edges], [neighbour, *vmem(x, whole_grid, *ends, rhs, *weights)]
        )
        corners = [corner]
    whole = (ANY, jax.ShapeDtypeStruct((32, 64, 128), F32))
    partial, whole_grid = call(
        middle_last,
        [whole, blocks(100)],
        args,
        [pltpu.VMEM((64, 32, 128), F32), dma((64,))],
        **work,
    )
    (out,) = call(
        outer_last,
        [whole],
        [neighbour, (ANY, partial), *vmem(whole_grid, *ends, rhs, *weights)],
        [pltpu.VMEM((4, 32, 128), F32), dma((4,))],
        {1: 0},
    )
    return out.reshape(old_conc.shape)


def solution(mesh):
    in_specs = (
        P(None, "tile", "slab", None),
        P("tile", "slab", None, None, None),
        P("tile", "slab", None, None),
        P("tile", "slab", None),
        P("tile", None, None),
        P(),
        P("tile", "slab", None),
        P("tile", "slab", None),
        P("tile", "slab", None),
    )
    out_specs = P(None, "tile", "slab", None)
    return jax.shard_map(body, mesh=mesh, in_specs=in_specs, out_specs=out_specs, check_vma=False)
```

```python
import functools

import jax
import jax.numpy as jnp
from jax import lax
from jax.experimental import pallas as pl
from jax.experimental.pallas import tpu as pltpu
from jax.sharding import PartitionSpec as P

BF16 = jnp.bfloat16
F32 = jnp.float32
WIDE = 10
CORNERS = (0, 7, 56, 63)
CORNER_HALOS = (0, 9, 90, 99)
INNER = tuple(b for b in range(64) if b not in CORNERS)

dot_t = functools.partial(
    lax.dot_general,
    dimension_numbers=(((1,), (1,)), ((), ())),
    preferred_element_type=F32,
)


def parity():
    return lax.rem(lax.axis_index("slab"), 2)


def even_tile():
    return lax.rem(lax.axis_index("tile"), 2) == 0


def far_is_real():
    slab = lax.axis_index("slab")
    return jnp.logical_or(slab == 1, slab == 2)


def above_is_real():
    return lax.axis_index("tile") > 0


def below_is_real():
    return lax.axis_index("tile") < lax.axis_size("tile") - 1


def only_if(real, value):
    return jnp.where(real, value, jnp.zeros_like(value))


def send_edges(x, to_near, to_far, to_mate, to_other):
    right, even = parity() == 0, even_tile()
    for r in range(8):
        first, last = x(r * 8), x(r * 8 + 7)
        to_near[r] = jnp.where(right, last, first)
        to_far[r] = jnp.where(right, first, last)
        top, bottom = x(r), x(56 + r)
        to_mate[r] = jnp.where(even, bottom, top)
        to_other[r] = jnp.where(even, top, bottom)


def bring_old(old, held, sems):
    copies = []
    for r in range(8):
        part = pl.ds(8 * r, 8)
        copies.append(pltpu.make_async_copy(old.at[:, part], held.at[:, part], sems.at[r]))
        copies[-1].start()
    return copies


def join(part0, part1, part2, part3, *after_and_whole):
    count, whole = part0.shape[0], after_and_whole[-1]
    for m, part in enumerate((part0, part1, part2, part3)):
        whole[pl.ds(m * count, count)] = part[...]


def prepare(old, stream, x, rhs, to_near, to_far, row, held, held_row, sems):
    copies = bring_old(old, held, sems)
    row_copy = pltpu.make_async_copy(stream, held_row, sems.at[8])
    row_copy.start()
    rows = held.reshape(32 * 64, 128)
    right = parity() == 0
    for r in range(8):
        copies[r].wait()
        for b in range(8 * r, 8 * r + 8):
            block = rows[pl.ds(b, 32, stride=64), :]
            rhs[b] = block
            x[b] = block.astype(BF16)
        first, last = x[8 * r], x[8 * r + 7]
        to_near[r] = jnp.where(right, last, first)
        to_far[r] = jnp.where(right, first, last)
    row_copy.wait()
    row[...] = held_row[...].astype(BF16)


def rows_to_send(x, from_near, from_far, to_mate, to_other):
    right, even = parity() == 0, even_tile()
    real = far_is_real()
    rows = []
    for r in (0, 7):
        near, far = from_near[r], only_if(real, from_far[r])
        rows.append([jnp.where(right, far, near), *(x[8 * r + c] for c in range(8)), jnp.where(right, near, far)])
    for i in range(WIDE):
        top, bottom = rows[0][i], rows[1][i]
        to_mate[i] = jnp.where(even, bottom, top)
        to_other[i] = jnp.where(even, top, bottom)


def pass_corners(from_near, from_far, to_mate, to_other):
    right, even = parity() == 0, even_tile()
    real = far_is_real()
    ends = []
    for r in (0, 7):
        near, far = from_near[r], only_if(real, from_far[r])
        ends.append((jnp.where(right, far, near), jnp.where(right, near, far)))
    for i in range(2):
        top, bottom = ends[0][i], ends[1][i]
        to_mate[i] = jnp.where(even, bottom, top)
        to_other[i] = jnp.where(even, top, bottom)


def at(b):
    return (b // 8 + 1) * WIDE + b % 8 + 1


def widen(grid, from_near, from_far, from_mate, from_other):
    right, even = parity() == 0, even_tile()
    real, above, below = far_is_real(), above_is_real(), below_is_real()
    for r in range(8):
        near, far = from_near[r], only_if(real, from_far[r])
        grid[(r + 1) * WIDE] = jnp.where(right, far, near)
        grid[(r + 1) * WIDE + 9] = jnp.where(right, near, far)
    count = from_mate.shape[0]
    first = (WIDE - count) // 2
    for c in range(count):
        mate, other = from_mate[c], from_other[c]
        grid[first + c] = only_if(above, jnp.where(even, other, mate))
        grid[90 + first + c] = only_if(below, jnp.where(even, mate, other))


def sweep(ids, upstream, rhs, upwind, diag, store):
    remainders = []
    for b, c in zip(ids[::2], ids[1::2], strict=True):
        both = jnp.concatenate([upstream(b), upstream(c)], axis=0)
        weights = [jnp.concatenate([upwind[d, k] for k in range(3)], axis=1) for d in (b, c)]
        coupled = dot_t(both, jnp.concatenate(weights, axis=0))
        remainders.append((rhs[b] - coupled[:32, :128]).astype(BF16))
        remainders.append((rhs[c] - coupled[32:, 128:]).astype(BF16))
    for i in range(0, len(ids), 2):
        both = jnp.concatenate(remainders[i : i + 2], axis=0)
        weights = jnp.concatenate([diag[ids[i]], diag[ids[i + 1]]], axis=0)
        conc = dot_t(both, weights)
        store(ids[i], conc[:32, :128])
        store(ids[i + 1], conc[32:, 128:])


def from_grid(neighbour, grid):
    return lambda b: jnp.concatenate([grid[neighbour[3 * b + k]] for k in range(3)], axis=1)


def row_of(well, parts):
    away = well ^ lax.axis_index("tile")
    place = (away // 4) % 4 * 4 + away // 16
    row = parts[0][place]
    for m in range(1, 4):
        row = jnp.where(away % 4 == m, parts[m][place], row)
    return row.astype(F32)


def load(neighbour_in, upwind_far, diag_far, upwind, diag, neighbour, sems):
    copies = [
        pltpu.make_async_copy(upwind_far, upwind, sems.at[0]),
        pltpu.make_async_copy(diag_far, diag, sems.at[1]),
    ]
    for copy in copies:
        copy.start()

    @pl.loop(0, neighbour.shape[0])
    def _(i):
        neighbour[i] = neighbour_in[i]

    for copy in copies:
        copy.wait()


def sweep_first(neighbour, x, near, far, mate, other, rhs, upwind, diag, x_next, grid):
    fill(grid, x, ())
    widen(grid, near, far, mate, other)

    def store(b, conc):
        x_next[b] = conc.astype(BF16)

    upstream = from_grid(neighbour, grid)
    for i in range(0, 64, 32):
        sweep(range(i, i + 32), upstream, rhs, upwind, diag, store)


def inject(
    neighbour, well, row, where, rate, rows0, rows1, rows2, rows3, x_in, rhs_in, grid, upwind, diag,
    x, rhs, to_near, to_far, to_mate, to_other,
):
    x[...] = x_in[...]
    rhs[...] = rhs_in[...]
    for p in range(4):
        b = where[0, 0, p]
        rhs[b] = rhs[b] + rate[0, 0, p] * row_of(row[well[0, 0, p]], (rows0, rows1, rows2, rows3))

    def store(b, conc):
        x[b] = conc.astype(BF16)

    sweep([where[0, 0, p] for p in range(4)], from_grid(neighbour, grid), rhs, upwind, diag, store)
    send_edges(lambda b: x[b], to_near, to_far, to_mate, to_other)


def fill(grid, x, corners):
    for b in range(64):
        if corners and b in CORNERS:
            grid[at(b)] = corners[0][CORNERS.index(b)]
        else:
            grid[at(b)] = x[b]


def middle(count, neighbour, x, *refs):
    corners, (near, far, mate, other, rhs, upwind, diag, x_next, grid) = refs[:count], refs[count:]
    fill(grid, x, corners)
    widen(grid, near, far, mate, other)

    def store(b, conc):
        x_next[b] = conc.astype(BF16)

    upstream = from_grid(neighbour, grid)
    for i in range(0, 60, 30):
        sweep(INNER[i : i + 30], upstream, rhs, upwind, diag, store)


def sweep_corners(neighbour, grid, mate, other, rhs, upwind, diag, store):
    even, above, below = even_tile(), above_is_real(), below_is_real()
    halos = [only_if(above, jnp.where(even, other[i], mate[i])) for i in range(2)]
    halos += [only_if(below, jnp.where(even, mate[i], other[i])) for i in range(2)]

    def upstream(b):
        i = CORNERS.index(b)
        slots = [neighbour[3 * b + k] for k in range(3)]
        return jnp.concatenate([jnp.where(n == CORNER_HALOS[i], halos[i], grid[n]) for n in slots], axis=1)

    sweep(CORNERS, upstream, rhs, upwind, diag, store)


def outer(neighbour, edges, grid, mate, other, rhs, upwind, diag, corners, to_near, to_far, to_mate, to_other):
    def store(b, conc):
        corners[CORNERS.index(b)] = conc.astype(BF16)

    sweep_corners(neighbour, grid, mate, other, rhs, upwind, diag, store)
    block = lambda b: corners[CORNERS.index(b)] if b in CORNERS else edges[b]
    send_edges(block, to_near, to_far, to_mate, to_other)


def middle_last(neighbour, x, corners, near, far, mate, other, rhs, upwind, diag, out, grid, held, sems):
    fill(grid, x, [corners])
    widen(grid, near, far, mate, other)
    copies = []

    def store(b, conc):
        held[b] = conc

    upstream = from_grid(neighbour, grid)
    for ids in (INNER[:24], INNER[24:48], INNER[48:]):
        sweep(ids, upstream, rhs, upwind, diag, store)
        for b in ids:
            copies.append(pltpu.make_async_copy(held.at[b], out.at[:, b], sems.at[b]))
            copies[-1].start()
    for copy in copies:
        copy.wait()


def outer_last(neighbour, partial, grid, mate, other, rhs, upwind, diag, out, held, sems):
    del partial

    def store(b, conc):
        held[CORNERS.index(b)] = conc

    sweep_corners(neighbour, grid, mate, other, rhs, upwind, diag, store)
    copies = [pltpu.make_async_copy(held.at[i], out.at[:, b], sems.at[i]) for i, b in enumerate(CORNERS)]
    for copy in copies:
        copy.start()
    for copy in copies:
        copy.wait()


VMEM, SMEM, ANY, HBM = (pl.BlockSpec(memory_space=m) for m in (pltpu.VMEM, pltpu.SMEM, pl.ANY, pltpu.HBM))

SMEM_FROM_HBM, SMEM_KEPT = "scalars", "kept scalars"


def call(kernel, outs, args, scratch=(), aliases=None, flops=0, moved=0):
    values = []
    for where, value in args:
        if where is VMEM:
            value = pltpu.with_memory_space_constraint(value, pltpu.VMEM)
        if where is SMEM_KEPT:
            value = pltpu.with_memory_space_constraint(value, pltpu.SMEM)
        if where in (HBM, SMEM_FROM_HBM):
            value = pltpu.with_memory_space_constraint(value, pltpu.HBM)
        values.append(value)
    shapes = []
    for where, s in outs:
        if where is VMEM:
            s = pltpu.VMEM(s.shape, s.dtype)
        if where is HBM:
            s = pltpu.HBM(s.shape, s.dtype)
        if where is SMEM:
            s = pltpu.SMEM(s.shape, s.dtype)
        shapes.append(s)
    return pl.pallas_call(
        kernel,
        out_shape=shapes,
        in_specs=[SMEM if isinstance(where, str) else where for where, _ in args],
        out_specs=[where for where, _ in outs],
        scratch_shapes=list(scratch),
        input_output_aliases=aliases or {},
        cost_estimate=pl.CostEstimate(flops=flops, bytes_accessed=moved, transcendentals=0),
        compiler_params=pltpu.CompilerParams(vmem_limit_bytes=6 * 2**20),
    )(*values)


def blocks(count, dtype=BF16):
    return VMEM, jax.ShapeDtypeStruct((count, 32, 128), dtype)


def body(
    old_conc, upwind, diag_inverse, neighbours, streams, injector_row, perf_well, perf_block, perf_rate
):
    tiles, slabs = lax.axis_size("tile"), lax.axis_size("slab")
    both = ("tile", "slab")
    on_chip = [(s, s ^ 1) for s in range(slabs)]
    far_pairs, mates, others = [], [], []
    for t in range(tiles):
        for s in range(slabs):
            here = t * slabs + s
            far_pairs.append((here, t * slabs + 3 - s if s in (1, 2) else (t ^ 1) * slabs + s))
            mates.append((here, (t ^ 1) * slabs + s))
            other = t - 1 if t % 2 == 0 else t + 1
            others.append((here, other * slabs + s if 0 <= other < tiles else t * slabs + (s ^ 1)))

    def vmem(*values):
        return [(VMEM, v) for v in values]

    def exchange(to_near, to_far, to_mate, to_other):
        from_far = lax.ppermute(to_far, both, far_pairs)
        from_near = lax.ppermute(to_near, "slab", on_chip)
        from_mate = lax.ppermute(to_mate, both, mates)
        from_other = lax.ppermute(to_other, both, others)
        return from_near, from_far, from_mate, from_other

    def exchange_corners(from_near, from_far):
        to_mate, to_other = call(pass_corners, [blocks(2)] * 2, vmem(from_near, from_far))
        return lax.ppermute(to_mate, both, mates), lax.ppermute(to_other, both, others)

    dma = pltpu.SemaphoreType.DMA
    held = pltpu.VMEM((32, 64, 128), F32)
    grid = pltpu.VMEM((100, 32, 128), BF16)
    edges = [blocks(8)] * 4
    neighbour = (SMEM, neighbours.reshape(-1))
    old = (HBM, old_conc.reshape(32, 64, 128))
    work = dict(flops=2 * 64 * 4 * 32 * 128 * 128, moved=9 * 2**20)

    def swaps(part, step):
        return [part] + [lax.ppermute(part, "tile", [(t, t ^ (m * step)) for t in range(tiles)]) for m in (1, 2, 3)]

    x, rhs, to_near, to_far, part = call(
        prepare,
        [blocks(64), blocks(64, F32), blocks(8), blocks(8), blocks(1)],
        [old, (HBM, streams)],
        [held, pltpu.VMEM((1, 32, 128), F32), dma((9,))],
        moved=4 * 2**20,
    )
    upwind_shape = jax.ShapeDtypeStruct((64, 3, 128, 128), BF16)
    diag_shape = jax.ShapeDtypeStruct((64, 128, 128), BF16)
    *weights, neighbour_here = call(
        load,
        [(VMEM, upwind_shape), (VMEM, diag_shape), (SMEM, jax.ShapeDtypeStruct((192,), jnp.int32))],
        [neighbour, (HBM, upwind.reshape(upwind_shape.shape)), (HBM, diag_inverse.reshape(diag_shape.shape))],
        [dma((2,))],
        moved=8 * 2**20,
    )
    neighbour = (SMEM_KEPT, neighbour_here)
    from_far = lax.ppermute(to_far, both, far_pairs)
    from_near = lax.ppermute(to_near, "slab", on_chip)
    to_mate, to_other = call(rows_to_send, [blocks(WIDE)] * 2, vmem(x, from_near, from_far))
    (part,) = call(join, [blocks(4)], vmem(*swaps(part, 16)))
    (part,) = call(join, [blocks(16)], vmem(*swaps(part, 4), weights[1], to_mate))
    rows = swaps(part, 1)

    got = from_near, from_far, lax.ppermute(to_mate, both, mates), lax.ppermute(to_other, both, others)

    wells = [(SMEM_FROM_HBM, v) for v in (perf_well, injector_row, perf_block, perf_rate)]
    x, whole_grid = call(
        sweep_first, [blocks(64), blocks(100)], [neighbour, *vmem(x, *got, rhs, *weights)], **work
    )
    x, rhs, *sent = call(
        inject,
        [blocks(64), blocks(64, F32), *edges],
        [neighbour, *wells, *vmem(*rows, x, rhs, whole_grid, *weights)],
    )
    corners = []
    for last in (False, True):
        got = exchange(*sent)
        ends = exchange_corners(*got[:2])
        args = [neighbour, *vmem(x, *corners, *got, rhs, *weights)]
        if last:
            break
        x, whole_grid = call(functools.partial(middle, len(corners)), [blocks(64), blocks(100)], args, **work)
        corner, *sent = call(
            outer, [blocks(4), *edges], [neighbour, *vmem(x, whole_grid, *ends, rhs, *weights)]
        )
        corners = [corner]
    whole = (ANY, jax.ShapeDtypeStruct((32, 64, 128), F32))
    partial, whole_grid = call(
        middle_last,
        [whole, blocks(100)],
        args,
        [pltpu.VMEM((64, 32, 128), F32), dma((64,))],
        **work,
    )
    (out,) = call(
        outer_last,
        [whole],
        [neighbour, (ANY, partial), *vmem(whole_grid, *ends, rhs, *weights)],
        [pltpu.VMEM((4, 32, 128), F32), dma((4,))],
        {1: 0},
    )
    return out.reshape(old_conc.shape)


def solution(mesh):
    in_specs = (
        P(None, "tile", "slab", None),
        P("tile", "slab", None, None, None),
        P("tile", "slab", None, None),
        P("tile", "slab", None),
        P("tile", None, None),
        P(),
        P("tile", "slab", None),
        P("tile", "slab", None),
        P("tile", "slab", None),
    )
    out_specs = P(None, "tile", "slab", None)
    return jax.shard_map(body, mesh=mesh, in_specs=in_specs, out_specs=out_specs, check_vma=False)
```

```python
import functools

import jax
import jax.numpy as jnp
from jax import lax
from jax.experimental import pallas as pl
from jax.experimental.pallas import tpu as pltpu
from jax.sharding import PartitionSpec as P

BF16 = jnp.bfloat16
F32 = jnp.float32
WIDE = 10
CORNERS = (0, 7, 56, 63)
CORNER_HALOS = (0, 9, 90, 99)
INNER = tuple(b for b in range(64) if b not in CORNERS)

dot_t = functools.partial(
    lax.dot_general,
    dimension_numbers=(((1,), (1,)), ((), ())),
    preferred_element_type=F32,
)


def parity():
    return lax.rem(lax.axis_index("slab"), 2)


def even_tile():
    return lax.rem(lax.axis_index("tile"), 2) == 0


def far_is_real():
    slab = lax.axis_index("slab")
    return jnp.logical_or(slab == 1, slab == 2)


def above_is_real():
    return lax.axis_index("tile") > 0


def below_is_real():
    return lax.axis_index("tile") < lax.axis_size("tile") - 1


def only_if(real, value):
    return jnp.where(real, value, jnp.zeros_like(value))


def send_edges(x, to_near, to_far, to_mate, to_other):
    right, even = parity() == 0, even_tile()
    for r in range(8):
        first, last = x(r * 8), x(r * 8 + 7)
        to_near[r] = jnp.where(right, last, first)
        to_far[r] = jnp.where(right, first, last)
        top, bottom = x(r), x(56 + r)
        to_mate[r] = jnp.where(even, bottom, top)
        to_other[r] = jnp.where(even, top, bottom)


def bring_old(old, held, sems):
    copies = []
    for r in range(8):
        part = pl.ds(8 * r, 8)
        copies.append(pltpu.make_async_copy(old.at[:, part], held.at[:, part], sems.at[r]))
        copies[-1].start()
    return copies


def join(part0, part1, part2, part3, *after_and_whole):
    count, whole = part0.shape[0], after_and_whole[-1]
    for m, part in enumerate((part0, part1, part2, part3)):
        whole[pl.ds(m * count, count)] = part[...]


def prepare(old, stream, x, rhs, to_near, to_far, row, held, held_row, sems):
    copies = bring_old(old, held, sems)
    row_copy = pltpu.make_async_copy(stream, held_row, sems.at[8])
    row_copy.start()
    rows = held.reshape(32 * 64, 128)
    right = parity() == 0
    for r in range(8):
        copies[r].wait()
        for b in range(8 * r, 8 * r + 8):
            block = rows[pl.ds(b, 32, stride=64), :]
            rhs[b] = block
            x[b] = block.astype(BF16)
        first, last = x[8 * r], x[8 * r + 7]
        to_near[r] = jnp.where(right, last, first)
        to_far[r] = jnp.where(right, first, last)
    row_copy.wait()
    row[...] = held_row[...].astype(BF16)


def rows_to_send(x, from_near, from_far, to_mate, to_other):
    right, even = parity() == 0, even_tile()
    real = far_is_real()
    rows = []
    for r in (0, 7):
        near, far = from_near[r], only_if(real, from_far[r])
        rows.append([jnp.where(right, far, near), *(x[8 * r + c] for c in range(8)), jnp.where(right, near, far)])
    for i in range(WIDE):
        top, bottom = rows[0][i], rows[1][i]
        to_mate[i] = jnp.where(even, bottom, top)
        to_other[i] = jnp.where(even, top, bottom)


def pass_corners(from_near, from_far, to_mate, to_other):
    right, even = parity() == 0, even_tile()
    real = far_is_real()
    ends = []
    for r in (0, 7):
        near, far = from_near[r], only_if(real, from_far[r])
        ends.append((jnp.where(right, far, near), jnp.where(right, near, far)))
    for i in range(2):
        top, bottom = ends[0][i], ends[1][i]
        to_mate[i] = jnp.where(even, bottom, top)
        to_other[i] = jnp.where(even, top, bottom)


def at(b):
    return (b // 8 + 1) * WIDE + b % 8 + 1


def widen(grid, from_near, from_far, from_mate, from_other):
    right, even = parity() == 0, even_tile()
    real, above, below = far_is_real(), above_is_real(), below_is_real()
    for r in range(8):
        near, far = from_near[r], only_if(real, from_far[r])
        grid[(r + 1) * WIDE] = jnp.where(right, far, near)
        grid[(r + 1) * WIDE + 9] = jnp.where(right, near, far)
    count = from_mate.shape[0]
    first = (WIDE - count) // 2
    for c in range(count):
        mate, other = from_mate[c], from_other[c]
        grid[first + c] = only_if(above, jnp.where(even, other, mate))
        grid[90 + first + c] = only_if(below, jnp.where(even, mate, other))


def sweep(ids, upstream, rhs, upwind, diag, store):
    remainders = []
    for b, c in zip(ids[::2], ids[1::2], strict=True):
        both = jnp.concatenate([upstream(b), upstream(c)], axis=0)
        weights = [jnp.concatenate([upwind[d, k] for k in range(3)], axis=1) for d in (b, c)]
        coupled = dot_t(both, jnp.concatenate(weights, axis=0))
        remainders.append((rhs[b] - coupled[:32, :128]).astype(BF16))
        remainders.append((rhs[c] - coupled[32:, 128:]).astype(BF16))
    for i in range(0, len(ids), 2):
        both = jnp.concatenate(remainders[i : i + 2], axis=0)
        weights = jnp.concatenate([diag[ids[i]], diag[ids[i + 1]]], axis=0)
        conc = dot_t(both, weights)
        store(ids[i], conc[:32, :128])
        store(ids[i + 1], conc[32:, 128:])


def from_grid(neighbour, grid):
    return lambda b: jnp.concatenate([grid[neighbour[3 * b + k]] for k in range(3)], axis=1)


def row_of(well, parts):
    away = well ^ lax.axis_index("tile")
    place = (away // 4) % 4 * 4 + away // 16
    row = parts[0][place]
    for m in range(1, 4):
        row = jnp.where(away % 4 == m, parts[m][place], row)
    return row.astype(F32)


def load(neighbour_in, upwind_far, diag_far, upwind, diag, neighbour, sems):
    copies = [
        pltpu.make_async_copy(upwind_far, upwind, sems.at[0]),
        pltpu.make_async_copy(diag_far, diag, sems.at[1]),
    ]
    for copy in copies:
        copy.start()

    @pl.loop(0, neighbour.shape[0])
    def _(i):
        neighbour[i] = neighbour_in[i]

    for copy in copies:
        copy.wait()


def sweep_first(neighbour, x, near, far, mate, other, rhs, upwind, diag, x_next, grid):
    fill(grid, x, ())
    widen(grid, near, far, mate, other)

    def store(b, conc):
        x_next[b] = conc.astype(BF16)

    upstream = from_grid(neighbour, grid)
    for i in range(0, 64, 32):
        sweep(range(i, i + 32), upstream, rhs, upwind, diag, store)


def inject(
    neighbour, well, row, where, rate, rows0, rows1, rows2, rows3, x_in, rhs_in, grid, upwind, diag,
    x, rhs, to_near, to_far, to_mate, to_other,
):
    x[...] = x_in[...]
    rhs[...] = rhs_in[...]
    for p in range(4):
        b = where[0, 0, p]
        rhs[b] = rhs[b] + rate[0, 0, p] * row_of(row[well[0, 0, p]], (rows0, rows1, rows2, rows3))

    def store(b, conc):
        x[b] = conc.astype(BF16)

    sweep([where[0, 0, p] for p in range(4)], from_grid(neighbour, grid), rhs, upwind, diag, store)
    send_edges(lambda b: x[b], to_near, to_far, to_mate, to_other)


def fill(grid, x, corners):
    for b in range(64):
        if corners and b in CORNERS:
            grid[at(b)] = corners[0][CORNERS.index(b)]
        else:
            grid[at(b)] = x[b]


def middle(count, neighbour, x, *refs):
    corners, (near, far, mate, other, rhs, upwind, diag, x_next, grid) = refs[:count], refs[count:]
    fill(grid, x, corners)
    widen(grid, near, far, mate, other)

    def store(b, conc):
        x_next[b] = conc.astype(BF16)

    upstream = from_grid(neighbour, grid)
    for i in range(0, 60, 30):
        sweep(INNER[i : i + 30], upstream, rhs, upwind, diag, store)


def sweep_corners(neighbour, grid, mate, other, rhs, upwind, diag, store):
    even, above, below = even_tile(), above_is_real(), below_is_real()
    halos = [only_if(above, jnp.where(even, other[i], mate[i])) for i in range(2)]
    halos += [only_if(below, jnp.where(even, mate[i], other[i])) for i in range(2)]

    def upstream(b):
        i = CORNERS.index(b)
        slots = [neighbour[3 * b + k] for k in range(3)]
        return jnp.concatenate([jnp.where(n == CORNER_HALOS[i], halos[i], grid[n]) for n in slots], axis=1)

    sweep(CORNERS, upstream, rhs, upwind, diag, store)


def outer(neighbour, edges, grid, mate, other, rhs, upwind, diag, corners, to_near, to_far, to_mate, to_other):
    def store(b, conc):
        corners[CORNERS.index(b)] = conc.astype(BF16)

    sweep_corners(neighbour, grid, mate, other, rhs, upwind, diag, store)
    block = lambda b: corners[CORNERS.index(b)] if b in CORNERS else edges[b]
    send_edges(block, to_near, to_far, to_mate, to_other)


def middle_last(neighbour, x, corners, near, far, mate, other, rhs, upwind, diag, out, grid, held, sems):
    fill(grid, x, [corners])
    widen(grid, near, far, mate, other)
    copies = []

    def store(b, conc):
        held[b] = conc

    upstream = from_grid(neighbour, grid)
    for ids in (INNER[:24], INNER[24:48], INNER[48:]):
        sweep(ids, upstream, rhs, upwind, diag, store)
        for b in ids:
            copies.append(pltpu.make_async_copy(held.at[b], out.at[:, b], sems.at[b]))
            copies[-1].start()
    for copy in copies:
        copy.wait()


def outer_last(neighbour, partial, grid, mate, other, rhs, upwind, diag, out, held, sems):
    del partial

    def store(b, conc):
        held[CORNERS.index(b)] = conc

    sweep_corners(neighbour, grid, mate, other, rhs, upwind, diag, store)
    copies = [pltpu.make_async_copy(held.at[i], out.at[:, b], sems.at[i]) for i, b in enumerate(CORNERS)]
    for copy in copies:
        copy.start()
    for copy in copies:
        copy.wait()


VMEM, SMEM, ANY, HBM = (pl.BlockSpec(memory_space=m) for m in (pltpu.VMEM, pltpu.SMEM, pl.ANY, pltpu.HBM))

SMEM_FROM_HBM, SMEM_KEPT = "scalars", "kept scalars"


def call(kernel, outs, args, scratch=(), aliases=None, flops=0, moved=0):
    values = []
    for where, value in args:
        if where is VMEM:
            value = pltpu.with_memory_space_constraint(value, pltpu.VMEM)
        if where is SMEM_KEPT:
            value = pltpu.with_memory_space_constraint(value, pltpu.SMEM)
        if where in (HBM, SMEM_FROM_HBM):
            value = pltpu.with_memory_space_constraint(value, pltpu.HBM)
        values.append(value)
    shapes = []
    for where, s in outs:
        if where is VMEM:
            s = pltpu.VMEM(s.shape, s.dtype)
        if where is HBM:
            s = pltpu.HBM(s.shape, s.dtype)
        if where is SMEM:
            s = pltpu.SMEM(s.shape, s.dtype)
        shapes.append(s)
    return pl.pallas_call(
        kernel,
        out_shape=shapes,
        in_specs=[SMEM if isinstance(where, str) else where for where, _ in args],
        out_specs=[where for where, _ in outs],
        scratch_shapes=list(scratch),
        input_output_aliases=aliases or {},
        cost_estimate=pl.CostEstimate(flops=flops, bytes_accessed=moved, transcendentals=0),
        compiler_params=pltpu.CompilerParams(vmem_limit_bytes=6 * 2**20),
    )(*values)


def blocks(count, dtype=BF16):
    return VMEM, jax.ShapeDtypeStruct((count, 32, 128), dtype)


def body(
    old_conc, upwind, diag_inverse, neighbours, streams, injector_row, perf_well, perf_block, perf_rate
):
    tiles, slabs = lax.axis_size("tile"), lax.axis_size("slab")
    both = ("tile", "slab")
    on_chip = [(s, s ^ 1) for s in range(slabs)]
    far_pairs, mates, others = [], [], []
    for t in range(tiles):
        for s in range(slabs):
            here = t * slabs + s
            far_pairs.append((here, t * slabs + 3 - s if s in (1, 2) else (t ^ 1) * slabs + s))
            mates.append((here, (t ^ 1) * slabs + s))
            other = t - 1 if t % 2 == 0 else t + 1
            others.append((here, other * slabs + s if 0 <= other < tiles else t * slabs + (s ^ 1)))

    def vmem(*values):
        return [(VMEM, v) for v in values]

    def exchange(to_near, to_far, to_mate, to_other):
        from_far = lax.ppermute(to_far, both, far_pairs)
        from_near = lax.ppermute(to_near, "slab", on_chip)
        from_mate = lax.ppermute(to_mate, both, mates)
        from_other = lax.ppermute(to_other, both, others)
        return from_near, from_far, from_mate, from_other

    def exchange_corners(from_near, from_far):
        to_mate, to_other = call(pass_corners, [blocks(2)] * 2, vmem(from_near, from_far))
        return lax.ppermute(to_mate, both, mates), lax.ppermute(to_other, both, others)

    dma = pltpu.SemaphoreType.DMA
    held = pltpu.VMEM((32, 64, 128), F32)
    grid = pltpu.VMEM((100, 32, 128), BF16)
    edges = [blocks(8)] * 4
    neighbour = (SMEM, neighbours.reshape(-1))
    old = (HBM, old_conc.reshape(32, 64, 128))
    work = dict(flops=2 * 64 * 4 * 32 * 128 * 128, moved=9 * 2**20)

    def swaps(part, step):
        return [part] + [lax.ppermute(part, "tile", [(t, t ^ (m * step)) for t in range(tiles)]) for m in (1, 2, 3)]

    x, rhs, to_near, to_far, part = call(
        prepare,
        [blocks(64), blocks(64, F32), blocks(8), blocks(8), blocks(1)],
        [old, (HBM, streams)],
        [held, pltpu.VMEM((1, 32, 128), F32), dma((9,))],
        moved=4 * 2**20,
    )
    upwind_shape = jax.ShapeDtypeStruct((64, 3, 128, 128), BF16)
    diag_shape = jax.ShapeDtypeStruct((64, 128, 128), BF16)
    *weights, neighbour_here = call(
        load,
        [(VMEM, upwind_shape), (VMEM, diag_shape), (SMEM, jax.ShapeDtypeStruct((192,), jnp.int32))],
        [neighbour, (HBM, upwind.reshape(upwind_shape.shape)), (HBM, diag_inverse.reshape(diag_shape.shape))],
        [dma((2,))],
        moved=8 * 2**20,
    )
    neighbour = (SMEM_KEPT, neighbour_here)
    from_far = lax.ppermute(to_far, both, far_pairs)
    from_near = lax.ppermute(to_near, "slab", on_chip)
    to_mate, to_other = call(rows_to_send, [blocks(WIDE)] * 2, vmem(x, from_near, from_far))
    got = from_near, from_far, lax.ppermute(to_mate, both, mates), lax.ppermute(to_other, both, others)
    (part,) = call(join, [blocks(4)], vmem(*swaps(part, 16), to_mate))
    (part,) = call(join, [blocks(16)], vmem(*swaps(part, 4), weights[1], *got[2:]))
    rows = swaps(part, 1)


    wells = [(SMEM_FROM_HBM, v) for v in (perf_well, injector_row, perf_block, perf_rate)]
    x, whole_grid = call(
        sweep_first, [blocks(64), blocks(100)], [neighbour, *vmem(x, *got, rhs, *weights)], **work
    )
    x, rhs, *sent = call(
        inject,
        [blocks(64), blocks(64, F32), *edges],
        [neighbour, *wells, *vmem(*rows, x, rhs, whole_grid, *weights)],
    )
    corners = []
    for last in (False, True):
        got = exchange(*sent)
        ends = exchange_corners(*got[:2])
        args = [neighbour, *vmem(x, *corners, *got, rhs, *weights)]
        if last:
            break
        x, whole_grid = call(functools.partial(middle, len(corners)), [blocks(64), blocks(100)], args, **work)
        corner, *sent = call(
            outer, [blocks(4), *edges], [neighbour, *vmem(x, whole_grid, *ends, rhs, *weights)]
        )
        corners = [corner]
    whole = (ANY, jax.ShapeDtypeStruct((32, 64, 128), F32))
    partial, whole_grid = call(
        middle_last,
        [whole, blocks(100)],
        args,
        [pltpu.VMEM((64, 32, 128), F32), dma((64,))],
        **work,
    )
    (out,) = call(
        outer_last,
        [whole],
        [neighbour, (ANY, partial), *vmem(whole_grid, *ends, rhs, *weights)],
        [pltpu.VMEM((4, 32, 128), F32), dma((4,))],
        {1: 0},
    )
    return out.reshape(old_conc.shape)


def solution(mesh):
    in_specs = (
        P(None, "tile", "slab", None),
        P("tile", "slab", None, None, None),
        P("tile", "slab", None, None),
        P("tile", "slab", None),
        P("tile", None, None),
        P(),
        P("tile", "slab", None),
        P("tile", "slab", None),
        P("tile", "slab", None),
    )
    out_specs = P(None, "tile", "slab", None)
    return jax.shard_map(body, mesh=mesh, in_specs=in_specs, out_specs=out_specs, check_vma=False)
```

```python
import functools

import jax
import jax.numpy as jnp
from jax import lax
from jax.experimental import pallas as pl
from jax.experimental.pallas import tpu as pltpu
from jax.sharding import PartitionSpec as P

BF16 = jnp.bfloat16
F32 = jnp.float32
WIDE = 10
CORNERS = (0, 7, 56, 63)
CORNER_HALOS = (0, 9, 90, 99)
INNER = tuple(b for b in range(64) if b not in CORNERS)

dot_t = functools.partial(
    lax.dot_general,
    dimension_numbers=(((1,), (1,)), ((), ())),
    preferred_element_type=F32,
)


def parity():
    return lax.rem(lax.axis_index("slab"), 2)


def even_tile():
    return lax.rem(lax.axis_index("tile"), 2) == 0


def far_is_real():
    slab = lax.axis_index("slab")
    return jnp.logical_or(slab == 1, slab == 2)


def above_is_real():
    return lax.axis_index("tile") > 0


def below_is_real():
    return lax.axis_index("tile") < lax.axis_size("tile") - 1


def only_if(real, value):
    return jnp.where(real, value, jnp.zeros_like(value))


def send_edges(x, to_near, to_far, to_mate, to_other):
    right, even = parity() == 0, even_tile()
    for r in range(8):
        first, last = x(r * 8), x(r * 8 + 7)
        to_near[r] = jnp.where(right, last, first)
        to_far[r] = jnp.where(right, first, last)
        top, bottom = x(r), x(56 + r)
        to_mate[r] = jnp.where(even, bottom, top)
        to_other[r] = jnp.where(even, top, bottom)


def bring_old(old, held, sems):
    copies = []
    for r in range(8):
        part = pl.ds(8 * r, 8)
        copies.append(pltpu.make_async_copy(old.at[:, part], held.at[:, part], sems.at[r]))
        copies[-1].start()
    return copies


def join(part0, part1, part2, part3, *after_and_whole):
    count, whole = part0.shape[0], after_and_whole[-1]
    for m, part in enumerate((part0, part1, part2, part3)):
        whole[pl.ds(m * count, count)] = part[...]


def prepare(old, stream, x, rhs, to_near, to_far, row, held, held_row, sems):
    copies = bring_old(old, held, sems)
    row_copy = pltpu.make_async_copy(stream, held_row, sems.at[8])
    row_copy.start()
    rows = held.reshape(32 * 64, 128)
    right = parity() == 0
    for r in range(8):
        copies[r].wait()
        for b in range(8 * r, 8 * r + 8):
            block = rows[pl.ds(b, 32, stride=64), :]
            rhs[b] = block
            x[b] = block.astype(BF16)
        first, last = x[8 * r], x[8 * r + 7]
        to_near[r] = jnp.where(right, last, first)
        to_far[r] = jnp.where(right, first, last)
    row_copy.wait()
    row[...] = held_row[...].astype(BF16)


def rows_to_send(x, from_near, from_far, after, to_mate, to_other):
    del after
    right, even = parity() == 0, even_tile()
    real = far_is_real()
    rows = []
    for r in (0, 7):
        near, far = from_near[r], only_if(real, from_far[r])
        rows.append([jnp.where(right, far, near), *(x[8 * r + c] for c in range(8)), jnp.where(right, near, far)])
    for i in range(WIDE):
        top, bottom = rows[0][i], rows[1][i]
        to_mate[i] = jnp.where(even, bottom, top)
        to_other[i] = jnp.where(even, top, bottom)


def pass_corners(from_near, from_far, to_mate, to_other):
    right, even = parity() == 0, even_tile()
    real = far_is_real()
    ends = []
    for r in (0, 7):
        near, far = from_near[r], only_if(real, from_far[r])
        ends.append((jnp.where(right, far, near), jnp.where(right, near, far)))
    for i in range(2):
        top, bottom = ends[0][i], ends[1][i]
        to_mate[i] = jnp.where(even, bottom, top)
        to_other[i] = jnp.where(even, top, bottom)


def at(b):
    return (b // 8 + 1) * WIDE + b % 8 + 1


def widen(grid, from_near, from_far, from_mate, from_other):
    right, even = parity() == 0, even_tile()
    real, above, below = far_is_real(), above_is_real(), below_is_real()
    for r in range(8):
        near, far = from_near[r], only_if(real, from_far[r])
        grid[(r + 1) * WIDE] = jnp.where(right, far, near)
        grid[(r + 1) * WIDE + 9] = jnp.where(right, near, far)
    count = from_mate.shape[0]
    first = (WIDE - count) // 2
    for c in range(count):
        mate, other = from_mate[c], from_other[c]
        grid[first + c] = only_if(above, jnp.where(even, other, mate))
        grid[90 + first + c] = only_if(below, jnp.where(even, mate, other))


def sweep(ids, upstream, rhs, upwind, diag, store):
    remainders = []
    for b, c in zip(ids[::2], ids[1::2], strict=True):
        both = jnp.concatenate([upstream(b), upstream(c)], axis=0)
        weights = [jnp.concatenate([upwind[d, k] for k in range(3)], axis=1) for d in (b, c)]
        coupled = dot_t(both, jnp.concatenate(weights, axis=0))
        remainders.append((rhs[b] - coupled[:32, :128]).astype(BF16))
        remainders.append((rhs[c] - coupled[32:, 128:]).astype(BF16))
    for i in range(0, len(ids), 2):
        both = jnp.concatenate(remainders[i : i + 2], axis=0)
        weights = jnp.concatenate([diag[ids[i]], diag[ids[i + 1]]], axis=0)
        conc = dot_t(both, weights)
        store(ids[i], conc[:32, :128])
        store(ids[i + 1], conc[32:, 128:])


def from_grid(neighbour, grid):
    return lambda b: jnp.concatenate([grid[neighbour[3 * b + k]] for k in range(3)], axis=1)


def row_of(well, parts):
    away = well ^ lax.axis_index("tile")
    place = (away // 4) % 4 * 4 + away // 16
    row = parts[0][place]
    for m in range(1, 4):
        row = jnp.where(away % 4 == m, parts[m][place], row)
    return row.astype(F32)


def load(neighbour_in, after, upwind_far, diag_far, upwind, diag, neighbour, sems):
    del after
    copies = [
        pltpu.make_async_copy(upwind_far, upwind, sems.at[0]),
        pltpu.make_async_copy(diag_far, diag, sems.at[1]),
    ]
    for copy in copies:
        copy.start()

    @pl.loop(0, neighbour.shape[0])
    def _(i):
        neighbour[i] = neighbour_in[i]

    for copy in copies:
        copy.wait()


def sweep_first(neighbour, x, near, far, mate, other, rhs, upwind, diag, x_next, grid):
    fill(grid, x, ())
    widen(grid, near, far, mate, other)

    def store(b, conc):
        x_next[b] = conc.astype(BF16)

    upstream = from_grid(neighbour, grid)
    for i in range(0, 64, 32):
        sweep(range(i, i + 32), upstream, rhs, upwind, diag, store)


def inject(
    neighbour, well, row, where, rate, rows0, rows1, rows2, rows3, x_in, rhs_in, grid, upwind, diag,
    x, rhs, to_near, to_far, to_mate, to_other,
):
    x[...] = x_in[...]
    rhs[...] = rhs_in[...]
    for p in range(4):
        b = where[0, 0, p]
        rhs[b] = rhs[b] + rate[0, 0, p] * row_of(row[well[0, 0, p]], (rows0, rows1, rows2, rows3))

    def store(b, conc):
        x[b] = conc.astype(BF16)

    sweep([where[0, 0, p] for p in range(4)], from_grid(neighbour, grid), rhs, upwind, diag, store)
    send_edges(lambda b: x[b], to_near, to_far, to_mate, to_other)


def fill(grid, x, corners):
    for b in range(64):
        if corners and b in CORNERS:
            grid[at(b)] = corners[0][CORNERS.index(b)]
        else:
            grid[at(b)] = x[b]


def middle(count, neighbour, x, *refs):
    corners, (near, far, mate, other, rhs, upwind, diag, x_next, grid) = refs[:count], refs[count:]
    fill(grid, x, corners)
    widen(grid, near, far, mate, other)

    def store(b, conc):
        x_next[b] = conc.astype(BF16)

    upstream = from_grid(neighbour, grid)
    for i in range(0, 60, 30):
        sweep(INNER[i : i + 30], upstream, rhs, upwind, diag, store)


def sweep_corners(neighbour, grid, mate, other, rhs, upwind, diag, store):
    even, above, below = even_tile(), above_is_real(), below_is_real()
    halos = [only_if(above, jnp.where(even, other[i], mate[i])) for i in range(2)]
    halos += [only_if(below, jnp.where(even, mate[i], other[i])) for i in range(2)]

    def upstream(b):
        i = CORNERS.index(b)
        slots = [neighbour[3 * b + k] for k in range(3)]
        return jnp.concatenate([jnp.where(n == CORNER_HALOS[i], halos[i], grid[n]) for n in slots], axis=1)

    sweep(CORNERS, upstream, rhs, upwind, diag, store)


def outer(neighbour, edges, grid, mate, other, rhs, upwind, diag, corners, to_near, to_far, to_mate, to_other):
    def store(b, conc):
        corners[CORNERS.index(b)] = conc.astype(BF16)

    sweep_corners(neighbour, grid, mate, other, rhs, upwind, diag, store)
    block = lambda b: corners[CORNERS.index(b)] if b in CORNERS else edges[b]
    send_edges(block, to_near, to_far, to_mate, to_other)


def middle_last(neighbour, x, corners, near, far, mate, other, rhs, upwind, diag, out, grid, held, sems):
    fill(grid, x, [corners])
    widen(grid, near, far, mate, other)
    copies = []

    def store(b, conc):
        held[b] = conc

    upstream = from_grid(neighbour, grid)
    for ids in (INNER[:24], INNER[24:48], INNER[48:]):
        sweep(ids, upstream, rhs, upwind, diag, store)
        for b in ids:
            copies.append(pltpu.make_async_copy(held.at[b], out.at[:, b], sems.at[b]))
            copies[-1].start()
    for copy in copies:
        copy.wait()


def outer_last(neighbour, partial, grid, mate, other, rhs, upwind, diag, out, held, sems):
    del partial

    def store(b, conc):
        held[CORNERS.index(b)] = conc

    sweep_corners(neighbour, grid, mate, other, rhs, upwind, diag, store)
    copies = [pltpu.make_async_copy(held.at[i], out.at[:, b], sems.at[i]) for i, b in enumerate(CORNERS)]
    for copy in copies:
        copy.start()
    for copy in copies:
        copy.wait()


VMEM, SMEM, ANY, HBM = (pl.BlockSpec(memory_space=m) for m in (pltpu.VMEM, pltpu.SMEM, pl.ANY, pltpu.HBM))

SMEM_FROM_HBM, SMEM_KEPT = "scalars", "kept scalars"


def call(kernel, outs, args, scratch=(), aliases=None, flops=0, moved=0):
    values = []
    for where, value in args:
        if where is VMEM:
            value = pltpu.with_memory_space_constraint(value, pltpu.VMEM)
        if where is SMEM_KEPT:
            value = pltpu.with_memory_space_constraint(value, pltpu.SMEM)
        if where in (HBM, SMEM_FROM_HBM):
            value = pltpu.with_memory_space_constraint(value, pltpu.HBM)
        values.append(value)
    shapes = []
    for where, s in outs:
        if where is VMEM:
            s = pltpu.VMEM(s.shape, s.dtype)
        if where is HBM:
            s = pltpu.HBM(s.shape, s.dtype)
        if where is SMEM:
            s = pltpu.SMEM(s.shape, s.dtype)
        shapes.append(s)
    return pl.pallas_call(
        kernel,
        out_shape=shapes,
        in_specs=[SMEM if isinstance(where, str) else where for where, _ in args],
        out_specs=[where for where, _ in outs],
        scratch_shapes=list(scratch),
        input_output_aliases=aliases or {},
        cost_estimate=pl.CostEstimate(flops=flops, bytes_accessed=moved, transcendentals=0),
        compiler_params=pltpu.CompilerParams(vmem_limit_bytes=6 * 2**20),
    )(*values)


def blocks(count, dtype=BF16):
    return VMEM, jax.ShapeDtypeStruct((count, 32, 128), dtype)


def body(
    old_conc, upwind, diag_inverse, neighbours, streams, injector_row, perf_well, perf_block, perf_rate
):
    tiles, slabs = lax.axis_size("tile"), lax.axis_size("slab")
    both = ("tile", "slab")
    on_chip = [(s, s ^ 1) for s in range(slabs)]
    far_pairs, mates, others = [], [], []
    for t in range(tiles):
        for s in range(slabs):
            here = t * slabs + s
            far_pairs.append((here, t * slabs + 3 - s if s in (1, 2) else (t ^ 1) * slabs + s))
            mates.append((here, (t ^ 1) * slabs + s))
            other = t - 1 if t % 2 == 0 else t + 1
            others.append((here, other * slabs + s if 0 <= other < tiles else t * slabs + (s ^ 1)))

    def vmem(*values):
        return [(VMEM, v) for v in values]

    def exchange(to_near, to_far, to_mate, to_other):
        from_far = lax.ppermute(to_far, both, far_pairs)
        from_near = lax.ppermute(to_near, "slab", on_chip)
        from_mate = lax.ppermute(to_mate, both, mates)
        from_other = lax.ppermute(to_other, both, others)
        return from_near, from_far, from_mate, from_other

    def exchange_corners(from_near, from_far):
        to_mate, to_other = call(pass_corners, [blocks(2)] * 2, vmem(from_near, from_far))
        return lax.ppermute(to_mate, both, mates), lax.ppermute(to_other, both, others)

    dma = pltpu.SemaphoreType.DMA
    held = pltpu.VMEM((32, 64, 128), F32)
    grid = pltpu.VMEM((100, 32, 128), BF16)
    edges = [blocks(8)] * 4
    neighbour = (SMEM, neighbours.reshape(-1))
    old = (HBM, old_conc.reshape(32, 64, 128))
    work = dict(flops=2 * 64 * 4 * 32 * 128 * 128, moved=9 * 2**20)

    def swaps(part, step):
        return [part] + [lax.ppermute(part, "tile", [(t, t ^ (m * step)) for t in range(tiles)]) for m in (1, 2, 3)]

    x, rhs, to_near, to_far, part = call(
        prepare,
        [blocks(64), blocks(64, F32), blocks(8), blocks(8), blocks(1)],
        [old, (HBM, streams)],
        [held, pltpu.VMEM((1, 32, 128), F32), dma((9,))],
        moved=4 * 2**20,
    )
    upwind_shape = jax.ShapeDtypeStruct((64, 3, 128, 128), BF16)
    diag_shape = jax.ShapeDtypeStruct((64, 128, 128), BF16)
    from_far = lax.ppermute(to_far, both, far_pairs)
    from_near = lax.ppermute(to_near, "slab", on_chip)
    (part,) = call(join, [blocks(4)], vmem(*swaps(part, 16)))
    to_mate, to_other = call(rows_to_send, [blocks(WIDE)] * 2, vmem(x, from_near, from_far, part))
    got = from_near, from_far, lax.ppermute(to_mate, both, mates), lax.ppermute(to_other, both, others)
    (part,) = call(join, [blocks(16)], vmem(*swaps(part, 4), *got[2:]))
    rows = swaps(part, 1)
    *weights, neighbour_here = call(
        load,
        [(VMEM, upwind_shape), (VMEM, diag_shape), (SMEM, jax.ShapeDtypeStruct((192,), jnp.int32))],
        [neighbour, (VMEM, part), (HBM, upwind.reshape(upwind_shape.shape)), (HBM, diag_inverse.reshape(diag_shape.shape))],
        [dma((2,))],
        moved=8 * 2**20,
    )
    neighbour = (SMEM_KEPT, neighbour_here)


    wells = [(SMEM_FROM_HBM, v) for v in (perf_well, injector_row, perf_block, perf_rate)]
    x, whole_grid = call(
        sweep_first, [blocks(64), blocks(100)], [neighbour, *vmem(x, *got, rhs, *weights)], **work
    )
    x, rhs, *sent = call(
        inject,
        [blocks(64), blocks(64, F32), *edges],
        [neighbour, *wells, *vmem(*rows, x, rhs, whole_grid, *weights)],
    )
    corners = []
    for last in (False, True):
        got = exchange(*sent)
        ends = exchange_corners(*got[:2])
        args = [neighbour, *vmem(x, *corners, *got, rhs, *weights)]
        if last:
            break
        x, whole_grid = call(functools.partial(middle, len(corners)), [blocks(64), blocks(100)], args, **work)
        corner, *sent = call(
            outer, [blocks(4), *edges], [neighbour, *vmem(x, whole_grid, *ends, rhs, *weights)]
        )
        corners = [corner]
    whole = (ANY, jax.ShapeDtypeStruct((32, 64, 128), F32))
    partial, whole_grid = call(
        middle_last,
        [whole, blocks(100)],
        args,
        [pltpu.VMEM((64, 32, 128), F32), dma((64,))],
        **work,
    )
    (out,) = call(
        outer_last,
        [whole],
        [neighbour, (ANY, partial), *vmem(whole_grid, *ends, rhs, *weights)],
        [pltpu.VMEM((4, 32, 128), F32), dma((4,))],
        {1: 0},
    )
    return out.reshape(old_conc.shape)


def solution(mesh):
    in_specs = (
        P(None, "tile", "slab", None),
        P("tile", "slab", None, None, None),
        P("tile", "slab", None, None),
        P("tile", "slab", None),
        P("tile", None, None),
        P(),
        P("tile", "slab", None),
        P("tile", "slab", None),
        P("tile", "slab", None),
    )
    out_specs = P(None, "tile", "slab", None)
    return jax.shard_map(body, mesh=mesh, in_specs=in_specs, out_specs=out_specs, check_vma=False)
```
